32 devices in a mesh: prompt: 4 (over y, core), seq: 2 (over x), blk: 4 (over z).
Axes of the slice: x: 2, y: 2, z: 4, core: 2. Of those that a mesh axis runs over, the one named last changes fastest.
Arguments:
- projections: bfloat16 [3, 4, 16, 4, 64, 128], P(None, None, None, 'blk', 'seq'), may hold values from -32 to 32
- residual: bfloat16 [4, 16, 4, 64, 128], P(None, None, 'blk', 'seq'), may hold values from -6 to 6
- out_proj: bfloat16 [2048, 2048], P('blk'), may hold values from -0.125 to 0.125
- modulation: float32 [3, 4, 2048], replicated, may hold values from -4 to 4
- final_weight: bfloat16 [2048, 64], replicated, may hold values from -0.125 to 0.125
- final_bias: float32 [64], replicated, may hold values from -3 to 3
- noisy_latents: float32 [4, 4, 64, 64], P(None, 'blk', 'seq'), may hold values from -6 to 6
- step_size: float32 [4], replicated, may hold values from 0.2 to 1
- conv_weight: bfloat16 [3, 3, 3, 16, 512], replicated, may hold values from -0.3125 to 0.3125
- conv_bias: float32 [512], replicated, may hold values from -3 to 3
Outputs:
- decoded: bfloat16 [16, 4, 512, 256], P(('prompt', 'blk'), None, None, 'seq'), parts along dimension 0
The draws below stay inside these ranges and needn't reach their ends.
There are 4 independent parts, one for each index of `prompt`. The reference program is written for one: setup_inputs(seed, part) draws one part's arguments, and reference() takes and returns one part's arrays. A program takes and returns all parts, laid end to end along the dimension named above; an argument that names none is the same for every part. Nothing has to cross between parts.
All inputs are finite; a program needn't handle non-finite values.
Results may differ from the reference program's by a relative error of at most 0.0075.
Values may be sent and summed in bfloat16 or wider, within the bound.
A program may use at most 64 MiB of HBM per device.

```python
import jax
import jax.numpy as jnp
from jax import lax

HEADS = 16
HEAD_DIM = 128
WIDTH = 2048
LATENT_CH = 16
PATCH = 2
PATCH_CH = 64
CONV_CH = 512
VIDEOS = 4
FRAMES = 4
PATCH_COLS = 32
PATCH_ROWS = 2
TOK_FRAME = 64
LAT_ROWS = 4
LAT_COLS = 64


def draw_projections(key, part):
    key = jax.random.fold_in(key, 7)
    base_key = jax.random.fold_in(key, 0)
    full_shape = (3, VIDEOS, HEADS, FRAMES, TOK_FRAME, HEAD_DIM)
    spread = 2.5 ** 0.5
    baseline = jnp.clip(jax.random.normal(base_key, full_shape, jnp.float32), -6.0, 6.0) * spread
    return baseline.astype(jnp.bfloat16)


def block_scale(stream_key, dims, cuts, low, high):
    level, own = 1.0, jax.random.fold_in(stream_key, 6)
    for dim, parts in cuts:
        heights = jnp.exp(jax.random.uniform(jax.random.fold_in(own, dim), (parts,), jnp.float32, low / len(cuts), high / len(cuts)))
        level = level * jnp.repeat(heights, dims[dim] // parts).reshape([-1 if axis == dim else 1 for axis in range(len(dims))])
    return level


def bell_draw(rng, shape, width, reach, pieces=(), kind=jnp.bfloat16):
    drawn = width * jax.random.normal(rng, shape, jnp.float32)
    if pieces:
        drawn = drawn * block_scale(rng, shape, pieces, -0.22, 0.18)
    return jnp.clip(drawn, -reach, reach).astype(kind)


def setup_inputs(seed: int = 0, part: int = 0) -> dict:
    keys = jax.random.split(jax.random.key(seed), 11)
    projections = draw_projections(jax.random.fold_in(keys[10], 71), part)
    residual = bell_draw(keys[1], (VIDEOS, HEADS, FRAMES, TOK_FRAME, HEAD_DIM), 1.0, 6.0, ((2, 4), (3, 2)))
    out_proj = bell_draw(keys[2], (WIDTH, WIDTH), WIDTH ** -0.5, 0.125, ((0, 4),))
    modulation = bell_draw(keys[3], (3, VIDEOS, WIDTH), 0.8, 4.0, (), jnp.float32)
    final_weight = bell_draw(keys[4], (WIDTH, PATCH_CH), WIDTH ** -0.5, 0.125)
    final_bias = bell_draw(keys[5], (PATCH_CH,), 0.5, 3.0, (), jnp.float32)
    noisy_latents = bell_draw(keys[6], (VIDEOS, FRAMES, TOK_FRAME, PATCH_CH), 1.0, 6.0, ((1, 4), (2, 2)), jnp.float32)
    step_size = jnp.clip(jax.random.uniform(keys[7], (VIDEOS,), jnp.float32, 0.2, 1.0), 0.2, 1.0)
    conv_weight = bell_draw(keys[8], (3, 3, 3, LATENT_CH, CONV_CH), (27 * LATENT_CH) ** -0.5, 0.3125)
    conv_bias = bell_draw(keys[9], (CONV_CH,), 0.5, 3.0, (), jnp.float32)
    return dict(projections=projections, residual=residual, out_proj=out_proj, modulation=modulation, final_weight=final_weight, final_bias=final_bias, noisy_latents=noisy_latents, step_size=step_size, conv_weight=conv_weight, conv_bias=conv_bias)


def attend_pair(operands):
    queries, key_rows, value_rows = operands
    scores = jnp.dot(queries, key_rows.T, preferred_element_type=jnp.float32) * HEAD_DIM ** (-0.5)
    row_max = lax.optimization_barrier(jnp.max(scores, axis=1, keepdims=True))
    exponents = jnp.exp(scores - row_max)
    totals = lax.optimization_barrier(jnp.sum(exponents, axis=1, keepdims=True))
    weighted = jnp.dot(exponents.astype(jnp.bfloat16), value_rows, preferred_element_type=jnp.float32)
    return (weighted / totals).astype(jnp.bfloat16)

def reference(projections, residual, out_proj, modulation, final_weight, final_bias, noisy_latents, step_size, conv_weight, conv_bias):
    pair_rows = projections.reshape(3, VIDEOS * HEADS, FRAMES * TOK_FRAME, HEAD_DIM)
    attended = lax.map(attend_pair, (pair_rows[0], pair_rows[1], pair_rows[2]))
    attended = attended.reshape(VIDEOS, HEADS, FRAMES, TOK_FRAME, HEAD_DIM)
    attended_tokens = jnp.transpose(attended, (0, 2, 3, 1, 4)).reshape(VIDEOS * FRAMES * TOK_FRAME, WIDTH)
    projected = jnp.dot(attended_tokens, out_proj, preferred_element_type=jnp.float32)
    projected = jnp.transpose(projected.reshape(VIDEOS, FRAMES, TOK_FRAME, HEADS, HEAD_DIM), (0, 3, 1, 2, 4))
    factors = modulation.reshape(3, VIDEOS, HEADS, 1, 1, HEAD_DIM)
    mixed = residual.astype(jnp.float32) + factors[2] * projected
    center = lax.optimization_barrier(jnp.mean(mixed, axis=(1, 4), keepdims=True))
    spread = lax.optimization_barrier(jnp.mean(jnp.square(mixed - center), axis=(1, 4), keepdims=True))
    normed = (mixed - center) * lax.rsqrt(spread + 1e-06)
    modulated = (normed * (1.0 + factors[1]) + factors[0]).astype(jnp.bfloat16)
    token_rows = jnp.transpose(modulated, (0, 2, 3, 1, 4)).reshape(VIDEOS * FRAMES * TOK_FRAME, WIDTH)
    prediction = jnp.dot(token_rows, final_weight, preferred_element_type=jnp.float32) + final_bias
    prediction = prediction.reshape(VIDEOS, FRAMES, TOK_FRAME, PATCH_CH)
    latents = ((noisy_latents + step_size[:, None, None, None] * prediction) / 0.476986).astype(jnp.bfloat16)
    latent_image = latents.reshape(VIDEOS, FRAMES, PATCH_ROWS, PATCH_COLS, LATENT_CH, PATCH, PATCH)
    latent_image = jnp.transpose(latent_image, (0, 1, 4, 2, 5, 3, 6)).reshape(VIDEOS, FRAMES, LATENT_CH, LAT_ROWS, LAT_COLS)
    padded = jnp.concatenate([latent_image[:, :1], latent_image[:, :1], latent_image], axis=1)
    padded = jnp.pad(padded, ((0, 0), (0, 0), (0, 0), (1, 1), (1, 1)))
    shifted = []
    for t_shift in range(3):
        for y_shift in range(3):
            for x_shift in range(3):
                shifted.append(padded[:, t_shift:t_shift + FRAMES, :, y_shift:y_shift + LAT_ROWS, x_shift:x_shift + LAT_COLS])
    columns = jnp.stack(shifted, axis=2).reshape(VIDEOS * FRAMES, 27 * LATENT_CH, LAT_ROWS * LAT_COLS)
    kernel = conv_weight.reshape(27 * LATENT_CH, CONV_CH)

    def decode_frame(frame_columns):
        result = jnp.dot(kernel.T, frame_columns, preferred_element_type=jnp.float32) + conv_bias[:, None]
        return result.astype(jnp.bfloat16)
    decoded = lax.map(decode_frame, columns)
    return decoded.reshape(VIDEOS, FRAMES, CONV_CH, LAT_ROWS * LAT_COLS)
```

```python
import functools
import math

import jax
import jax.numpy as jnp
from jax import lax
from jax.experimental import pallas as pl
from jax.experimental.pallas import tpu as pltpu
from jax.sharding import PartitionSpec as P

HEADS = 16
LATENT_CH = 16
PATCH = 2
ROWS_DEV = 1
PATCH_COLS = 32


def extended_2(cells, sides, width):
    for axis, dim in sides:
        count = lax.axis_size(axis)
        ends = count - 1
        head = lax.slice_in_dim(cells, 0, width, axis=dim)
        tail = lax.slice_in_dim(cells, cells.shape[dim] - width, cells.shape[dim], axis=dim)
        cells = jnp.concatenate(
            [
                lax.ppermute(tail, axis, [(i, (i + 1) % count) for i in range(ends)]),
                cells,
                lax.ppermute(head, axis, [((i + 1) % count, i) for i in range(ends)]),
            ],
            axis=dim,
        )
    return cells


def initial_state(queries):
    rows_shape = queries.shape[:2]
    return (
        jnp.full(rows_shape, -jnp.inf, jnp.float32),
        jnp.zeros(rows_shape, jnp.float32),
        jnp.zeros(queries.shape, jnp.float32),
    )


def attend_keys(partial_value, queries, key_part, value_part):
    key_rows = key_part.reshape(key_part.shape[0], -1, key_part.shape[-1])
    value_rows = value_part.reshape(value_part.shape[0], -1, value_part.shape[-1])
    key_count = key_rows.shape[1]
    block_len = math.gcd(key_count, 512)
    scale_factor = queries.shape[-1] ** (-0.5)

    def one_block(offset, state):
        running_max, running_sum, accumulated = state
        key_block = lax.dynamic_slice_in_dim(key_rows, offset * block_len, block_len, 1)
        value_block = lax.dynamic_slice_in_dim(value_rows, offset * block_len, block_len, 1)
        scores = (
            jnp.einsum("nqd,nkd->nqk", queries, key_block, preferred_element_type=jnp.float32)
            * scale_factor
        )
        new_max = jnp.maximum(running_max, jnp.max(scores, axis=2))
        rescale = jnp.exp(running_max - new_max)
        weights = jnp.exp(scores - new_max[:, :, None])
        new_sum = running_sum * rescale + jnp.sum(weights, axis=2)
        product = jnp.einsum(
            "nqk,nkd->nqd",
            weights.astype(jnp.bfloat16),
            value_block,
            preferred_element_type=jnp.float32,
        )
        return (new_max, new_sum, accumulated * rescale[:, :, None] + product)

    return lax.fori_loop(0, key_count // block_len, one_block, partial_value)


def finish_state(partial_value):
    return (partial_value[2] / partial_value[1][:, :, None]).astype(jnp.bfloat16)[:, None]


def convolve(time_stack, conv_weight, conv_bias):
    row_count = time_stack.shape[3] - 2
    col_count = time_stack.shape[4]
    widened = jnp.pad(time_stack, ((0, 0), (0, 0), (0, 0), (0, 0), (1, 1)))
    shifted = []
    for t_shift in range(3):
        for y_shift in range(3):
            for x_shift in range(3):
                shifted.append(
                    widened[
                        :, t_shift, :, y_shift : y_shift + row_count, x_shift : x_shift + col_count
                    ]
                )
    columns = jnp.stack(shifted, axis=1).reshape(
        time_stack.shape[0], 27 * time_stack.shape[2], row_count * col_count
    )
    kernel = conv_weight.reshape(27 * time_stack.shape[2], conv_weight.shape[-1])
    result = (
        jnp.einsum("ko,bkp->bop", kernel, columns, preferred_element_type=jnp.float32)
        + conv_bias[None, :, None]
    )
    return result.astype(jnp.bfloat16)


def body(
    projections,
    residual,
    out_proj,
    modulation,
    final_weight,
    final_bias,
    noisy_latents,
    step_size,
    conv_weight,
    conv_bias,
):
    videos_here = projections.shape[1]
    tok_here = projections.shape[4]
    head_size = projections.shape[5]
    seq_count = lax.axis_size("seq")
    pair_major = projections.reshape(
        3, seq_count, videos_here * HEADS // seq_count, 1, tok_here, head_size
    )
    kv_frames = lax.all_gather(pair_major[1:], "blk", axis=3, tiled=True)
    received = (
        lax.all_to_all(pair_major[:1], "seq", split_axis=1, concat_axis=4, tiled=True),
        lax.all_to_all(kv_frames, "seq", split_axis=1, concat_axis=4, tiled=True),
    )
    queries = received[0][0, 0, :, 0]
    partial_value = attend_keys(
        initial_state(queries), queries, received[1][0, 0], received[1][1, 0]
    )
    attended = finish_state(partial_value)
    token_major = lax.all_to_all(attended, "seq", split_axis=2, concat_axis=0, tiled=True)
    token_major = token_major.reshape(videos_here, HEADS, 1, tok_here, head_size)
    width_all = HEADS * head_size
    token_rows = jnp.transpose(token_major, (0, 2, 3, 1, 4)).reshape(
        videos_here * tok_here, width_all
    )
    projected = jnp.dot(
        token_rows,
        lax.all_gather(out_proj, "blk", axis=0, tiled=True),
        preferred_element_type=jnp.float32,
    )
    projected = jnp.transpose(
        projected.reshape(videos_here, 1, tok_here, HEADS, head_size), (0, 3, 1, 2, 4)
    )
    factors = modulation.reshape(3, videos_here, HEADS, 1, 1, head_size)
    mixed = residual.astype(jnp.float32) + factors[2] * projected
    center = jnp.mean(mixed, axis=(1, 4), keepdims=True)
    spread = jnp.mean(jnp.square(mixed - center), axis=(1, 4), keepdims=True)
    normed = (mixed - center) * lax.rsqrt(spread + 1e-06)
    modulated = (normed * (1.0 + factors[1]) + factors[0]).astype(jnp.bfloat16)
    out_weight = final_weight.reshape(HEADS, head_size, final_weight.shape[1])
    prediction = (
        jnp.einsum("vhftd,hdo->vfto", modulated, out_weight, preferred_element_type=jnp.float32)
        + final_bias
    )
    latents = ((noisy_latents + step_size[:, None, None, None] * prediction) / 0.476986).astype(
        jnp.bfloat16
    )
    latent_image = latents.reshape(videos_here, 1, ROWS_DEV, PATCH_COLS, LATENT_CH, PATCH, PATCH)
    latent_image = jnp.transpose(latent_image, (0, 1, 4, 2, 5, 3, 6))
    latent_image = latent_image.reshape(
        videos_here, 1, LATENT_CH, PATCH * ROWS_DEV, PATCH * PATCH_COLS
    )
    tile_frames = lax.all_to_all(latent_image, "blk", split_axis=0, concat_axis=1, tiled=True)[0]
    extended = extended_2(tile_frames, (("seq", 2),), 1)
    padded = jnp.concatenate([extended[:1], extended[:1], extended], axis=0)
    frame_total = tile_frames.shape[0]
    time_stack = jnp.stack(
        [padded[0:frame_total], padded[1 : frame_total + 1], padded[2 : frame_total + 2]], axis=1
    )
    decoded = convolve(time_stack, conv_weight, conv_bias)[None]
    return decoded


def fits(mesh):
    return mesh.shape["seq"] == 2 and mesh.shape["blk"] == 4 and mesh.shape["prompt"] == 4


def dot(lhs, rhs, lhs_dim=1, rhs_dim=0):
    return lax.dot_general(
        lhs, rhs, (((lhs_dim,), (rhs_dim,)), ((), ())), preferred_element_type=jnp.float32
    )


def fused_kernel(
    proj,
    res_in,
    out_w,
    noisy_in,
    mod,
    final_w,
    final_b,
    step,
    conv_w,
    conv_b,
    out,
    qkv,
    res,
    noisy,
    rows,
    att,
    part_out,
    part_in,
    mixed,
    normal,
    image,
    halo,
    strip,
    spread,
    columns,
    bias,
    factors,
    qkv_send,
    qkv_recv,
    res_send,
    res_recv,
    noisy_send,
    noisy_recv,
    row_send,
    row_recv,
    share_send,
    share_recv,
    part_send,
    part_recv,
    halo_sem,
    local_sem,
):
    p, s, b = lax.axis_index("prompt"), lax.axis_index("seq"), lax.axis_index("blk")
    other = 1 - s
    blks = [lax.rem(b + d, 4) for d in range(4)]
    froms = [lax.rem(b + 4 - d, 4) for d in range(4)]
    seqs = [s, other]
    prompts = [lax.rem(p + d, 4) for d in range(4)]
    prompt_froms = [lax.rem(p + 4 - d, 4) for d in range(4)]
    pairs = [(db, ds) for db in (2, 1, 3, 0) for ds in (0, 1) if (db, ds) != (0, 0)]

    barrier = pltpu.get_barrier_semaphore()
    for db, ds in pairs:
        pl.semaphore_signal(barrier, inc=1, device_id=(p, seqs[ds], blks[db]), device_id_type=pl.DeviceIdType.MESH)
    for dp in (1, 2, 3):
        pl.semaphore_signal(barrier, inc=1, device_id=(prompts[dp], s, b), device_id_type=pl.DeviceIdType.MESH)
    pl.semaphore_wait(barrier, 10)

    def remote(src, dst, send, recv, target):
        return pltpu.make_async_remote_copy(
            src_ref=src,
            dst_ref=dst,
            send_sem=send,
            recv_sem=recv,
            device_id=target,
            device_id_type=pl.DeviceIdType.MESH,
        )

    def row_slot(group, quarter):
        return rows.at[pl.ds(pl.multiple_of(group * 256 + quarter * 64, 64), 64)]

    def row_copy(db, source):
        return remote(out_w.at[s, p], row_slot(source, p), row_send.at[db], row_recv.at[source], (p, s, blks[db]))

    def share_copy(group, dp, source):
        return remote(
            row_slot(group, source),
            row_slot(group, source),
            share_send.at[group, dp],
            share_recv.at[group, source],
            (prompts[dp], s, b),
        )

    def qkv_copy(g, db, ds, frame, row):
        return remote(
            proj.at[:, blks[db], g, seqs[ds]],
            qkv.at[:, g, :, frame, row],
            qkv_send.at[g, db, ds],
            qkv_recv.at[g, frame, row],
            (p, seqs[ds], blks[db]),
        )

    def res_copy(db, frame):
        return remote(res_in.at[blks[db]], res.at[:, frame], res_send.at[db], res_recv.at[frame], (p, s, blks[db]))

    def noisy_copy(db, frame):
        return remote(noisy_in.at[blks[db]], noisy.at[frame], noisy_send.at[db], noisy_recv.at[frame], (p, s, blks[db]))

    for db in (2, 1, 3):
        row_copy(db, b).start()
    for g in range(4):
        for db, ds in pairs:
            qkv_copy(g, db, ds, b, s).start()
    for db in (2, 1, 3):
        noisy_copy(db, b).start()
        res_copy(db, b).start()
    own = [
        pltpu.make_async_copy(proj.at[:, b, g, s], qkv.at[:, g, :, b, s], local_sem.at[g]) for g in range(4)
    ]
    own.append(pltpu.make_async_copy(res_in.at[b], res.at[:, b], local_sem.at[4]))
    own.append(pltpu.make_async_copy(noisy_in.at[b], noisy.at[b], local_sem.at[5]))
    for quarter in range(4):
        own.append(pltpu.make_async_copy(out_w.at[s, quarter], row_slot(b, quarter), local_sem.at[6 + quarter]))
    for copy in own:
        copy.start()

    for half in range(2):
        at_row = lax.broadcasted_iota(jnp.int32, (128, 768), 0)
        at_col = lax.broadcasted_iota(jnp.int32, (128, 768), 1)
        same = (at_row >> 5) == ((at_col >> 6) & 3)
        place = (at_col & 63) == 2 * (at_row & 31) + (half + 1) - (at_col >> 8)
        spread[half * 128 : half * 128 + 128, :] = jnp.where(same & place, 1.0, 0.0).astype(jnp.bfloat16)
    for k in range(3):
        video = lax.broadcasted_iota(jnp.int32, (4, 2048), 0)
        factors[k : k + 1, :] = jnp.sum(jnp.where(video == b, mod[k], 0.0), axis=0, keepdims=True)
    bias[...] = jnp.broadcast_to(conv_b[...], (128, 512)).T

    for db in (1, 3, 2):
        row_copy(db, froms[db]).wait_recv()
        for dp in (1, 2, 3):
            share_copy(froms[db], dp, p).start()

    scale = 128 ** (-0.5)
    for g in range(4):
        own[g].wait()
        for db, ds in pairs:
            qkv_copy(g, db, ds, froms[db], seqs[ds]).wait_recv()
        for k in range(2):
            q = qkv[0, g, k].reshape(256, 128)
            key = qkv[1, g, k].reshape(256, 128)
            value = qkv[2, g, k].reshape(256, 128)
            scores = dot(q, key, 1, 1) * scale
            weights = jnp.exp(scores - jnp.max(scores, axis=1, keepdims=True))
            totals = jnp.sum(weights, axis=1, keepdims=True)
            result = (dot(weights.astype(jnp.bfloat16), value) / totals).astype(jnp.bfloat16)
            at = (g * 2 + k) * 128
            for f in range(4):
                for i in range(2):
                    att[i, f * 32 : f * 32 + 32, at : at + 128] = result[f * 64 + i * 32 : f * 64 + i * 32 + 32]

    for quarter in range(4):
        own[6 + quarter].wait()
    for db in (1, 3, 2):
        for dp in (1, 2, 3):
            share_copy(froms[db], dp, prompt_froms[dp]).wait_recv()

    def part_copy(c):
        cols = pl.ds(c * 512, 512)
        return remote(part_out.at[:, cols], part_in.at[:, cols], part_send.at[c], part_recv.at[c], (p, other, b))

    for c in range(4):
        part_out[:, c * 512 : c * 512 + 512] = dot(att[other], rows[:, c * 512 : c * 512 + 512]).astype(jnp.bfloat16)
        part_copy(c).start()
    own[4].wait()
    for db in (1, 3, 2):
        res_copy(db, froms[db]).wait_recv()

    total = jnp.zeros((128, 128), jnp.float32)
    for c in range(4):
        mine = dot(att[s], rows[:, c * 512 : c * 512 + 512])
        part_copy(c).wait_recv()
        for k in range(4):
            h = c * 4 + k
            at = h * 128
            projected = mine[:, k * 128 : k * 128 + 128] + part_in[:, at : at + 128].astype(jnp.float32)
            value = res[h].reshape(128, 128).astype(jnp.float32) + factors[2:3, at : at + 128] * projected
            mixed[:, at : at + 128] = value
            total = total + value
    center = jnp.sum(total, axis=1, keepdims=True) * (1.0 / 2048)
    total = jnp.zeros((128, 128), jnp.float32)
    for h in range(16):
        total = total + jnp.square(mixed[:, h * 128 : h * 128 + 128] - center)
    inverse = lax.rsqrt(jnp.sum(total, axis=1, keepdims=True) * (1.0 / 2048) + 1e-06)
    for h in range(16):
        at = h * 128
        normed = (mixed[:, at : at + 128] - center) * inverse
        normal[:, at : at + 128] = (
            normed * (1.0 + factors[1:2, at : at + 128]) + factors[0:1, at : at + 128]
        ).astype(jnp.bfloat16)
    prediction = dot(normal[...], final_w[...]) + final_b[...]
    own[5].wait()
    for db in (1, 3, 2):
        noisy_copy(db, froms[db]).wait_recv()
    latents = ((noisy[...].reshape(128, 64) + step[b] * prediction) / 0.476986).astype(jnp.bfloat16)

    to = lax.broadcasted_iota(jnp.int32, (64, 64), 0)
    channel = lax.broadcasted_iota(jnp.int32, (64, 64), 1)
    pick = jnp.where(channel == 4 * (to & 15) + (to >> 4), 1.0, 0.0).astype(jnp.bfloat16)
    image[...] = dot(pick, latents, 1, 1).astype(jnp.bfloat16)
    edge = remote(
        image.at[pl.ds(pl.multiple_of(32 * other, 32), 32)], halo, halo_sem.at[0], halo_sem.at[1], (p, other, b)
    )
    edge.start()
    for half in range(2):
        lanes = slice(half * 128, half * 128 + 128)
        strip[16:32, lanes] = image[half * 16 : half * 16 + 16, :]
        strip[32:48, lanes] = image[32 + half * 16 : 32 + half * 16 + 16, :]
    edge.wait_recv()
    for half in range(2):
        lanes = slice(half * 128, half * 128 + 128)
        beside = halo[half * 16 : half * 16 + 16, :].astype(jnp.float32)
        strip[0:16, lanes] = jnp.where(s == 1, beside, 0.0).astype(jnp.bfloat16)
        strip[48:64, lanes] = jnp.where(s == 0, beside, 0.0).astype(jnp.bfloat16)
    shifted = dot(strip[...], spread[...])
    for e in range(3):
        for f in range(4):
            lanes = slice(e * 256 + f * 64, e * 256 + f * 64 + 64)
            block = jnp.concatenate([shifted[0:48, lanes], shifted[16:64, lanes]], axis=1).astype(jnp.bfloat16)
            for t in range(3):
                for frame in range(4):
                    if max(frame + t - 2, 0) == f:
                        for y in range(3):
                            at = (t * 9 + y * 3 + e) * 16
                            columns[at : at + 16, frame * 128 : frame * 128 + 128] = block[y * 16 : y * 16 + 16]
    for f in range(4):
        decoded = dot(conv_w[...], columns[:, f * 128 : f * 128 + 128], 0, 0)
        out[f] = (decoded + bias[...]).astype(jnp.bfloat16)

    for db in (1, 3, 2):
        row_copy(db, b).wait_send()
        res_copy(db, b).wait_send()
        noisy_copy(db, b).wait_send()
        for dp in (1, 2, 3):
            share_copy(froms[db], dp, p).wait_send()
    for g in range(4):
        for db, ds in pairs:
            qkv_copy(g, db, ds, b, s).wait_send()
    for c in range(4):
        part_copy(c).wait_send()
    edge.wait_send()


def fused(
    projections,
    residual,
    out_proj,
    modulation,
    final_weight,
    final_bias,
    noisy_latents,
    step_size,
    conv_weight,
    conv_bias,
):
    anywhere = pl.BlockSpec(memory_space=pl.ANY)
    vmem = pl.BlockSpec(memory_space=pltpu.VMEM)
    smem = pl.BlockSpec(memory_space=pltpu.SMEM)
    half, full = jnp.bfloat16, jnp.float32
    dma = pltpu.SemaphoreType.DMA
    decoded = pl.pallas_call(
        fused_kernel,
        out_shape=jax.ShapeDtypeStruct((4, 512, 128), half),
        in_specs=[anywhere] * 4 + [vmem] * 3 + [smem] + [vmem] * 2,
        out_specs=vmem,
        scratch_shapes=[
            pltpu.VMEM((3, 4, 2, 4, 2, 32, 128), half),
            pltpu.VMEM((16, 4, 32, 128), half),
            pltpu.VMEM((4, 32, 64), full),
            pltpu.VMEM((1024, 2048), half),
            pltpu.VMEM((2, 128, 1024), half),
            pltpu.VMEM((128, 2048), half),
            pltpu.VMEM((128, 2048), half),
            pltpu.VMEM((128, 2048), full),
            pltpu.VMEM((128, 2048), half),
            pltpu.VMEM((64, 128), half),
            pltpu.VMEM((32, 128), half),
            pltpu.VMEM((64, 256), half),
            pltpu.VMEM((256, 768), half),
            pltpu.VMEM((432, 512), half),
            pltpu.VMEM((512, 128), full),
            pltpu.VMEM((8, 2048), full),
            dma((4, 4, 2)),
            dma((4, 4, 2)),
            dma((4,)),
            dma((4,)),
            dma((4,)),
            dma((4,)),
            dma((4,)),
            dma((4,)),
            dma((4, 4)),
            dma((4, 4)),
            dma((4,)),
            dma((4,)),
            dma((2,)),
            dma((10,)),
        ],
        compiler_params=pltpu.CompilerParams(
            collective_id=0, has_side_effects=True, vmem_limit_bytes=40 * 1024 * 1024
        ),
    )(
        projections.reshape(3, 4, 4, 2, 2, 32, 128),
        residual.reshape(4, 16, 32, 128),
        out_proj.reshape(2, 4, 64, 2048),
        noisy_latents.reshape(4, 32, 64),
        modulation,
        final_weight,
        final_bias.reshape(1, 64),
        step_size,
        conv_weight.reshape(432, 512),
        conv_bias.reshape(1, 512),
    )
    return decoded[None]


def solution(mesh):
    return jax.shard_map(
        fused if fits(mesh) else body,
        mesh=mesh,
        in_specs=(
            P(None, None, None, "blk", "seq", None),
            P(None, None, "blk", "seq", None),
            P("blk", None),
            P(),
            P(),
            P(),
            P(None, "blk", "seq", None),
            P(),
            P(),
            P(),
        ),
        out_specs=P(("prompt", "blk"), None, None, "seq"),
        check_vma=False,
    )
```

```python
import functools
import math

import jax
import jax.numpy as jnp
from jax import lax
from jax.experimental import pallas as pl
from jax.experimental.pallas import tpu as pltpu
from jax.sharding import PartitionSpec as P

HEADS = 16
LATENT_CH = 16
PATCH = 2
ROWS_DEV = 1
PATCH_COLS = 32


def extended_2(cells, sides, width):
    for axis, dim in sides:
        count = lax.axis_size(axis)
        ends = count - 1
        head = lax.slice_in_dim(cells, 0, width, axis=dim)
        tail = lax.slice_in_dim(cells, cells.shape[dim] - width, cells.shape[dim], axis=dim)
        cells = jnp.concatenate(
            [
                lax.ppermute(tail, axis, [(i, (i + 1) % count) for i in range(ends)]),
                cells,
                lax.ppermute(head, axis, [((i + 1) % count, i) for i in range(ends)]),
            ],
            axis=dim,
        )
    return cells


def initial_state(queries):
    rows_shape = queries.shape[:2]
    return (
        jnp.full(rows_shape, -jnp.inf, jnp.float32),
        jnp.zeros(rows_shape, jnp.float32),
        jnp.zeros(queries.shape, jnp.float32),
    )


def attend_keys(partial_value, queries, key_part, value_part):
    key_rows = key_part.reshape(key_part.shape[0], -1, key_part.shape[-1])
    value_rows = value_part.reshape(value_part.shape[0], -1, value_part.shape[-1])
    key_count = key_rows.shape[1]
    block_len = math.gcd(key_count, 512)
    scale_factor = queries.shape[-1] ** (-0.5)

    def one_block(offset, state):
        running_max, running_sum, accumulated = state
        key_block = lax.dynamic_slice_in_dim(key_rows, offset * block_len, block_len, 1)
        value_block = lax.dynamic_slice_in_dim(value_rows, offset * block_len, block_len, 1)
        scores = (
            jnp.einsum("nqd,nkd->nqk", queries, key_block, preferred_element_type=jnp.float32)
            * scale_factor
        )
        new_max = jnp.maximum(running_max, jnp.max(scores, axis=2))
        rescale = jnp.exp(running_max - new_max)
        weights = jnp.exp(scores - new_max[:, :, None])
        new_sum = running_sum * rescale + jnp.sum(weights, axis=2)
        product = jnp.einsum(
            "nqk,nkd->nqd",
            weights.astype(jnp.bfloat16),
            value_block,
            preferred_element_type=jnp.float32,
        )
        return (new_max, new_sum, accumulated * rescale[:, :, None] + product)

    return lax.fori_loop(0, key_count // block_len, one_block, partial_value)


def finish_state(partial_value):
    return (partial_value[2] / partial_value[1][:, :, None]).astype(jnp.bfloat16)[:, None]


def convolve(time_stack, conv_weight, conv_bias):
    row_count = time_stack.shape[3] - 2
    col_count = time_stack.shape[4]
    widened = jnp.pad(time_stack, ((0, 0), (0, 0), (0, 0), (0, 0), (1, 1)))
    shifted = []
    for t_shift in range(3):
        for y_shift in range(3):
            for x_shift in range(3):
                shifted.append(
                    widened[
                        :, t_shift, :, y_shift : y_shift + row_count, x_shift : x_shift + col_count
                    ]
                )
    columns = jnp.stack(shifted, axis=1).reshape(
        time_stack.shape[0], 27 * time_stack.shape[2], row_count * col_count
    )
    kernel = conv_weight.reshape(27 * time_stack.shape[2], conv_weight.shape[-1])
    result = (
        jnp.einsum("ko,bkp->bop", kernel, columns, preferred_element_type=jnp.float32)
        + conv_bias[None, :, None]
    )
    return result.astype(jnp.bfloat16)


def body(
    projections,
    residual,
    out_proj,
    modulation,
    final_weight,
    final_bias,
    noisy_latents,
    step_size,
    conv_weight,
    conv_bias,
):
    videos_here = projections.shape[1]
    tok_here = projections.shape[4]
    head_size = projections.shape[5]
    seq_count = lax.axis_size("seq")
    pair_major = projections.reshape(
        3, seq_count, videos_here * HEADS // seq_count, 1, tok_here, head_size
    )
    kv_frames = lax.all_gather(pair_major[1:], "blk", axis=3, tiled=True)
    received = (
        lax.all_to_all(pair_major[:1], "seq", split_axis=1, concat_axis=4, tiled=True),
        lax.all_to_all(kv_frames, "seq", split_axis=1, concat_axis=4, tiled=True),
    )
    queries = received[0][0, 0, :, 0]
    partial_value = attend_keys(
        initial_state(queries), queries, received[1][0, 0], received[1][1, 0]
    )
    attended = finish_state(partial_value)
    token_major = lax.all_to_all(attended, "seq", split_axis=2, concat_axis=0, tiled=True)
    token_major = token_major.reshape(videos_here, HEADS, 1, tok_here, head_size)
    width_all = HEADS * head_size
    token_rows = jnp.transpose(token_major, (0, 2, 3, 1, 4)).reshape(
        videos_here * tok_here, width_all
    )
    projected = jnp.dot(
        token_rows,
        lax.all_gather(out_proj, "blk", axis=0, tiled=True),
        preferred_element_type=jnp.float32,
    )
    projected = jnp.transpose(
        projected.reshape(videos_here, 1, tok_here, HEADS, head_size), (0, 3, 1, 2, 4)
    )
    factors = modulation.reshape(3, videos_here, HEADS, 1, 1, head_size)
    mixed = residual.astype(jnp.float32) + factors[2] * projected
    center = jnp.mean(mixed, axis=(1, 4), keepdims=True)
    spread = jnp.mean(jnp.square(mixed - center), axis=(1, 4), keepdims=True)
    normed = (mixed - center) * lax.rsqrt(spread + 1e-06)
    modulated = (normed * (1.0 + factors[1]) + factors[0]).astype(jnp.bfloat16)
    out_weight = final_weight.reshape(HEADS, head_size, final_weight.shape[1])
    prediction = (
        jnp.einsum("vhftd,hdo->vfto", modulated, out_weight, preferred_element_type=jnp.float32)
        + final_bias
    )
    latents = ((noisy_latents + step_size[:, None, None, None] * prediction) / 0.476986).astype(
        jnp.bfloat16
    )
    latent_image = latents.reshape(videos_here, 1, ROWS_DEV, PATCH_COLS, LATENT_CH, PATCH, PATCH)
    latent_image = jnp.transpose(latent_image, (0, 1, 4, 2, 5, 3, 6))
    latent_image = latent_image.reshape(
        videos_here, 1, LATENT_CH, PATCH * ROWS_DEV, PATCH * PATCH_COLS
    )
    tile_frames = lax.all_to_all(latent_image, "blk", split_axis=0, concat_axis=1, tiled=True)[0]
    extended = extended_2(tile_frames, (("seq", 2),), 1)
    padded = jnp.concatenate([extended[:1], extended[:1], extended], axis=0)
    frame_total = tile_frames.shape[0]
    time_stack = jnp.stack(
        [padded[0:frame_total], padded[1 : frame_total + 1], padded[2 : frame_total + 2]], axis=1
    )
    decoded = convolve(time_stack, conv_weight, conv_bias)[None]
    return decoded


def fits(mesh):
    return mesh.shape["seq"] == 2 and mesh.shape["blk"] == 4 and mesh.shape["prompt"] == 4


def dot(lhs, rhs, lhs_dim=1, rhs_dim=0):
    return lax.dot_general(
        lhs, rhs, (((lhs_dim,), (rhs_dim,)), ((), ())), preferred_element_type=jnp.float32
    )


def fused_kernel(
    proj,
    res_in,
    out_w,
    noisy_in,
    mod_in,
    final_in,
    final_b_in,
    conv_in,
    conv_b_in,
    step,
    out,
    qkv,
    res,
    noisy,
    rows,
    att,
    projected,
    centred,
    summary_out,
    summary_in,
    strip,
    spread,
    columns,
    bias,
    factors,
    mod,
    final_w,
    final_b,
    conv_w,
    conv_b,
    conv_t,
    qkv_send,
    qkv_recv,
    res_send,
    res_recv,
    noisy_send,
    noisy_recv,
    row_send,
    row_recv,
    forward_send,
    share_send,
    share_recv,
    att_send,
    att_recv,
    summary_sem,
    local_sem,
):
    p, s, b = lax.axis_index("prompt"), lax.axis_index("seq"), lax.axis_index("blk")
    other = 1 - s
    blks = [lax.rem(b + d, 4) for d in range(4)]
    froms = [lax.rem(b + 4 - d, 4) for d in range(4)]
    seqs = [s, other]
    prompts = [lax.rem(p + d, 4) for d in range(4)]
    prompt_froms = [lax.rem(p + 4 - d, 4) for d in range(4)]
    pairs = [(db, ds) for db in (2, 1, 3, 0) for ds in (0, 1) if (db, ds) != (0, 0)]

    barrier = pltpu.get_barrier_semaphore()
    for db, ds in pairs:
        pl.semaphore_signal(barrier, inc=1, device_id=(p, seqs[ds], blks[db]), device_id_type=pl.DeviceIdType.MESH)
    for dp in (1, 2, 3):
        pl.semaphore_signal(barrier, inc=1, device_id=(prompts[dp], s, b), device_id_type=pl.DeviceIdType.MESH)
    pl.semaphore_wait(barrier, 10)

    def remote(src, dst, send, recv, target):
        return pltpu.make_async_remote_copy(
            src_ref=src,
            dst_ref=dst,
            send_sem=send,
            recv_sem=recv,
            device_id=target,
            device_id_type=pl.DeviceIdType.MESH,
        )

    near = b + 1 - 2 * lax.rem(b, 2)
    inner = 2 - b // 2
    outer = 3 * (1 - b // 2)

    def row_slot(group, quarter):
        return rows.at[pl.ds(pl.multiple_of(group * 512 + quarter * 128, 128), 128)]

    def own_rows(quarter):
        return out_w.at[quarter, :, pl.ds(pl.multiple_of(s * 1024, 1024), 1024)]

    def row_copy(k, target, source):
        return remote(own_rows(p), row_slot(source, p), row_send.at[k], row_recv.at[source], (p, s, target))

    def forward_copy(k, source):
        slot = row_slot(source, p)
        return remote(slot, slot, forward_send.at[k], row_recv.at[source], (p, s, near))

    def share_copy(group, dp, source):
        return remote(
            row_slot(group, source),
            row_slot(group, source),
            share_send.at[group, dp],
            share_recv.at[group, source],
            (prompts[dp], s, b),
        )

    def qkv_copy(g, db, ds, frame, row):
        return remote(
            proj.at[:, blks[db], g, seqs[ds]],
            qkv.at[:, g, :, frame, row],
            qkv_send.at[g, db, ds],
            qkv_recv.at[g, frame, row],
            (p, seqs[ds], blks[db]),
        )

    def res_copy(db, ds, frame, row):
        return remote(
            res_in.at[blks[db], seqs[ds]],
            res.at[:, frame, row],
            res_send.at[db, ds],
            res_recv.at[frame, row],
            (p, seqs[ds], blks[db]),
        )

    def noisy_copy(db, ds, frame, row):
        return remote(
            noisy_in.at[blks[db]],
            noisy.at[frame, row],
            noisy_send.at[db, ds],
            noisy_recv.at[frame, row],
            (p, seqs[ds], blks[db]),
        )

    row_copy(0, inner, b).start()
    row_copy(1, near, b).start()
    for g in range(4):
        for db, ds in pairs:
            qkv_copy(g, db, ds, b, s).start()
    for db, ds in pairs:
        noisy_copy(db, ds, b, s).start()
        res_copy(db, ds, b, s).start()
    own = [
        pltpu.make_async_copy(proj.at[:, b, g, s], qkv.at[:, g, :, b, s], local_sem.at[g]) for g in range(4)
    ]
    own.append(pltpu.make_async_copy(res_in.at[b, s], res.at[:, b, s], local_sem.at[4]))
    own.append(pltpu.make_async_copy(noisy_in.at[b], noisy.at[b, s], local_sem.at[5]))
    for quarter in range(4):
        own.append(pltpu.make_async_copy(own_rows(quarter), row_slot(b, quarter), local_sem.at[6 + quarter]))
    tables = ((mod_in, mod), (final_in, final_w), (final_b_in, final_b), (conv_in, conv_w), (conv_b_in, conv_b))
    for k, (src, dst) in enumerate(tables):
        own.append(pltpu.make_async_copy(src, dst, local_sem.at[10 + k]))
    for copy in own:
        copy.start()

    for half in range(2):
        at_row = lax.broadcasted_iota(jnp.int32, (256, 768), 0)
        at_col = lax.broadcasted_iota(jnp.int32, (256, 768), 1)
        same = (at_row >> 6) == ((at_col >> 6) & 3)
        place = (at_col & 63) == 2 * (at_row & 31) + (half + 1) - (at_col >> 8)
        spread[half * 256 : half * 256 + 256, :] = jnp.where(same & place, 1.0, 0.0).astype(jnp.bfloat16)
    for copy in own[10:]:
        copy.wait()
    for k in range(3):
        video = lax.broadcasted_iota(jnp.int32, (4, 2048), 0)
        factors[k : k + 1, :] = jnp.sum(jnp.where(video == b, mod[k], 0.0), axis=0, keepdims=True)
    bias[...] = jnp.broadcast_to(conv_b[...], (128, 512)).T

    conv_t[...] = conv_w[...].T

    def split(value):
        high = value.astype(jnp.bfloat16)
        return high.astype(jnp.float32), value - high.astype(jnp.float32)

    row = lax.broadcasted_iota(jnp.int32, (8, 1024), 0)
    tilts = []
    moved = final_b[...]
    for half in range(2):
        lanes = slice(half * 1024, half * 1024 + 1024)
        high, low = split(1.0 + factors[1:2, lanes])
        shift_high, shift_low = split(factors[0:1, lanes])
        parts = jnp.where(row == 0, high, 0.0) + jnp.where(row == 1, low, 0.0)
        parts = parts + jnp.where(row == 2, shift_high, 0.0) + jnp.where(row == 3, shift_low, 0.0)
        sums = dot(parts.astype(jnp.bfloat16), final_w[:, lanes], 1, 1)
        tilts.append(sums[0:1] + sums[1:2])
        moved = moved + sums[2:3] + sums[3:4]
    tilt_mine = jnp.where(s == 0, tilts[0], tilts[1])
    tilt_other = jnp.where(s == 0, tilts[1], tilts[0])

    for k, source in enumerate((near, inner, outer)):
        row_copy(0, near, source).wait_recv()
        if k > 0:

            @pl.when(lax.rem(b, 3) != 0)
            def _(k=k, source=source):
                forward_copy(k - 1, source).start()

        for dp in (1, 2, 3):
            share_copy(source, dp, p).start()

    def att_copy(g, side):
        cols = att.at[:, pl.ds(pl.multiple_of((4 * g + 2 * side) * 128, 256), 256)]
        return remote(cols, cols, att_send.at[g], att_recv.at[g], (p, other, b))

    scale = 128 ** (-0.5)
    for g in range(4):
        own[g].wait()
        for db, ds in pairs:
            qkv_copy(g, db, ds, froms[db], seqs[ds]).wait_recv()
        for k in range(2):
            q = qkv[0, g, k].reshape(256, 128)
            key = qkv[1, g, k].reshape(256, 128)
            value = qkv[2, g, k].reshape(256, 128)
            scores = dot(q, key, 1, 1) * scale
            weights = jnp.exp(scores - jnp.max(scores, axis=1, keepdims=True))
            totals = jnp.sum(weights, axis=1, keepdims=True)
            result = (dot(weights.astype(jnp.bfloat16), value) / totals).astype(jnp.bfloat16)
            att[:, pl.ds(pl.multiple_of((4 * g + 2 * s + k) * 128, 128), 128)] = result
        att_copy(g, s).start()
        if g == 2:
            for quarter in range(4):
                own[6 + quarter].wait()
            for source in (near, inner, outer):
                for dp in (1, 2, 3):
                    share_copy(source, dp, prompt_froms[dp]).wait_recv()
            for done in range(3):
                att_copy(done, other).wait_recv()
            for n in range(2):
                lanes = slice(n * 512, n * 512 + 512)
                projected[:, lanes] = dot(att[:, 0:1536], rows[0:1536, lanes])

    own[4].wait()
    for db, ds in pairs:
        res_copy(db, ds, froms[db], seqs[ds]).wait_recv()
    att_copy(3, other).wait_recv()
    total = jnp.zeros((256, 128), jnp.float32)
    for n in range(2):
        last = dot(att[:, 1536:2048], rows[1536:2048, n * 512 : n * 512 + 512])
        for k in range(4):
            h = n * 4 + k
            lanes = slice(h * 128, h * 128 + 128)
            value = projected[:, lanes] + last[:, k * 128 : k * 128 + 128]
            gate = jnp.where(s == 0, factors[2:3, lanes], factors[2:3, 1024 + h * 128 : 1152 + h * 128])
            value = res[h].reshape(256, 128).astype(jnp.float32) + gate * value
            projected[:, lanes] = value
            total = total + value
    center = jnp.sum(total, axis=1, keepdims=True) * (1.0 / 1024)
    total = jnp.zeros((256, 128), jnp.float32)
    for h in range(8):
        lanes = slice(h * 128, h * 128 + 128)
        away = projected[:, lanes] - center
        total = total + jnp.square(away)
        gain = jnp.where(s == 0, factors[1:2, lanes], factors[1:2, 1024 + h * 128 : 1152 + h * 128])
        centred[:, lanes] = (away * (1.0 + gain)).astype(jnp.bfloat16)
    squares = jnp.sum(total, axis=1, keepdims=True)
    weighted = dot(centred[...], final_w[:, pl.ds(pl.multiple_of(s * 1024, 1024), 1024)], 1, 1)
    summary_out[:, 0:64] = weighted
    lane = lax.broadcasted_iota(jnp.int32, (256, 64), 1)
    summary_out[:, 64:128] = jnp.where(lane == 0, center, jnp.where(lane == 1, squares, 0.0))
    summary = remote(summary_out, summary_in, summary_sem.at[0], summary_sem.at[1], (p, other, b))
    summary.start()
    own[5].wait()
    for db, ds in pairs:
        noisy_copy(db, ds, froms[db], seqs[ds]).wait_recv()
    start = noisy[...].reshape(256, 64)
    summary.wait_recv()
    center_other = summary_in[:, 64:65]
    squares = squares + summary_in[:, 65:66]
    apart = (center - center_other) * 0.5
    inverse = lax.rsqrt(squares * (1.0 / 2048) + jnp.square(apart) + 1e-06)
    weighted = weighted + summary_in[:, 0:64] + apart * (tilt_mine - tilt_other)
    prediction = inverse * weighted + moved
    latents = ((start + step[b] * prediction) / 0.476986).astype(jnp.bfloat16)

    to = lax.broadcasted_iota(jnp.int32, (64, 64), 0)
    channel = lax.broadcasted_iota(jnp.int32, (64, 64), 1)
    pick = jnp.where(channel == 4 * (to & 15) + (to >> 4), 1.0, 0.0).astype(jnp.bfloat16)
    image = dot(pick, latents, 1, 1)
    row_of = (lax.broadcasted_iota(jnp.int32, (16, 256), 1) >> 5) & 1
    for r in range(4):
        here = row_of == s + (r + 1) // 2 - 1
        for half in range(2):
            at = (1 - r % 2) * 32 + half * 16
            kept = jnp.where(here, image[at : at + 16], 0.0).astype(jnp.bfloat16)
            strip[r * 16 : r * 16 + 16, half * 256 : half * 256 + 256] = kept
    shifted = dot(strip[...], spread[...])
    for e in range(3):
        for f in range(4):
            lanes = slice(e * 256 + f * 64, e * 256 + f * 64 + 64)
            block = jnp.concatenate([shifted[0:48, lanes], shifted[16:64, lanes]], axis=1).astype(jnp.bfloat16)
            for t in range(3):
                for frame in range(4):
                    if max(frame + t - 2, 0) == f:
                        for y in range(3):
                            at = (t * 9 + y * 3 + e) * 16
                            columns[at : at + 16, frame * 128 : frame * 128 + 128] = block[y * 16 : y * 16 + 16]
    for f in range(4):
        decoded = dot(conv_t[...], columns[:, f * 128 : f * 128 + 128])
        out[f] = (decoded + bias[...]).astype(jnp.bfloat16)

    for k, source in enumerate((near, inner, outer)):
        if k < 2:
            row_copy(k, near, b).wait_send()
        else:

            @pl.when(lax.rem(b, 3) != 0)
            def _():
                forward_copy(0, inner).wait_send()
                forward_copy(1, outer).wait_send()

        for dp in (1, 2, 3):
            share_copy(source, dp, p).wait_send()
    for db, ds in pairs:
        res_copy(db, ds, b, s).wait_send()
        noisy_copy(db, ds, b, s).wait_send()
        for g in range(4):
            qkv_copy(g, db, ds, b, s).wait_send()
    for g in range(4):
        att_copy(g, s).wait_send()
    summary.wait_send()


def fused(
    projections,
    residual,
    out_proj,
    modulation,
    final_weight,
    final_bias,
    noisy_latents,
    step_size,
    conv_weight,
    conv_bias,
):
    anywhere = pl.BlockSpec(memory_space=pl.ANY)
    vmem = pl.BlockSpec(memory_space=pltpu.VMEM)
    smem = pl.BlockSpec(memory_space=pltpu.SMEM)
    half, full = jnp.bfloat16, jnp.float32
    dma = pltpu.SemaphoreType.DMA
    decoded = pl.pallas_call(
        fused_kernel,
        out_shape=jax.ShapeDtypeStruct((4, 512, 128), half),
        in_specs=[anywhere] * 9 + [smem],
        out_specs=vmem,
        scratch_shapes=[
            pltpu.VMEM((3, 4, 2, 4, 2, 32, 128), half),
            pltpu.VMEM((8, 4, 2, 32, 128), half),
            pltpu.VMEM((4, 2, 32, 64), full),
            pltpu.VMEM((2048, 1024), half),
            pltpu.VMEM((256, 2048), half),
            pltpu.VMEM((256, 1024), full),
            pltpu.VMEM((256, 1024), half),
            pltpu.VMEM((256, 128), full),
            pltpu.VMEM((256, 128), full),
            pltpu.VMEM((64, 512), half),
            pltpu.VMEM((512, 768), half),
            pltpu.VMEM((432, 512), half),
            pltpu.VMEM((512, 128), full),
            pltpu.VMEM((8, 2048), full),
            pltpu.VMEM((3, 4, 2048), full),
            pltpu.VMEM((64, 2048), half),
            pltpu.VMEM((1, 64), full),
            pltpu.VMEM((432, 512), half),
            pltpu.VMEM((1, 512), full),
            pltpu.VMEM((512, 432), half),
            dma((4, 4, 2)),
            dma((4, 4, 2)),
            dma((4, 2)),
            dma((4, 2)),
            dma((4, 2)),
            dma((4, 2)),
            dma((2,)),
            dma((4,)),
            dma((2,)),
            dma((4, 4)),
            dma((4, 4)),
            dma((4,)),
            dma((4,)),
            dma((2,)),
            dma((15,)),
        ],
        compiler_params=pltpu.CompilerParams(
            collective_id=0, has_side_effects=True, vmem_limit_bytes=60 * 1024 * 1024
        ),
    )(
        projections.reshape(3, 4, 4, 2, 2, 32, 128),
        residual.reshape(4, 2, 8, 32, 128),
        out_proj.reshape(4, 128, 2048),
        noisy_latents.reshape(4, 32, 64),
        modulation,
        final_weight.T,
        final_bias.reshape(1, 64),
        conv_weight.reshape(432, 512),
        conv_bias.reshape(1, 512),
        step_size,
    )
    return decoded[None]


def solution(mesh):
    return jax.shard_map(
        fused if fits(mesh) else body,
        mesh=mesh,
        in_specs=(
            P(None, None, None, "blk", "seq", None),
            P(None, None, "blk", "seq", None),
            P("blk", None),
            P(),
            P(),
            P(),
            P(None, "blk", "seq", None),
            P(),
            P(),
            P(),
        ),
        out_specs=P(("prompt", "blk"), None, None, "seq"),
        check_vma=False,
    )
```

```python
import functools
import math

import jax
import jax.numpy as jnp
from jax import lax
from jax.experimental import pallas as pl
from jax.experimental.pallas import tpu as pltpu
from jax.sharding import PartitionSpec as P

HEADS = 16
LATENT_CH = 16
PATCH = 2
ROWS_DEV = 1
PATCH_COLS = 32


def extended_2(cells, sides, width):
    for axis, dim in sides:
        count = lax.axis_size(axis)
        ends = count - 1
        head = lax.slice_in_dim(cells, 0, width, axis=dim)
        tail = lax.slice_in_dim(cells, cells.shape[dim] - width, cells.shape[dim], axis=dim)
        cells = jnp.concatenate(
            [
                lax.ppermute(tail, axis, [(i, (i + 1) % count) for i in range(ends)]),
                cells,
                lax.ppermute(head, axis, [((i + 1) % count, i) for i in range(ends)]),
            ],
            axis=dim,
        )
    return cells


def initial_state(queries):
    rows_shape = queries.shape[:2]
    return (
        jnp.full(rows_shape, -jnp.inf, jnp.float32),
        jnp.zeros(rows_shape, jnp.float32),
        jnp.zeros(queries.shape, jnp.float32),
    )


def attend_keys(partial_value, queries, key_part, value_part):
    key_rows = key_part.reshape(key_part.shape[0], -1, key_part.shape[-1])
    value_rows = value_part.reshape(value_part.shape[0], -1, value_part.shape[-1])
    key_count = key_rows.shape[1]
    block_len = math.gcd(key_count, 512)
    scale_factor = queries.shape[-1] ** (-0.5)

    def one_block(offset, state):
        running_max, running_sum, accumulated = state
        key_block = lax.dynamic_slice_in_dim(key_rows, offset * block_len, block_len, 1)
        value_block = lax.dynamic_slice_in_dim(value_rows, offset * block_len, block_len, 1)
        scores = (
            jnp.einsum("nqd,nkd->nqk", queries, key_block, preferred_element_type=jnp.float32)
            * scale_factor
        )
        new_max = jnp.maximum(running_max, jnp.max(scores, axis=2))
        rescale = jnp.exp(running_max - new_max)
        weights = jnp.exp(scores - new_max[:, :, None])
        new_sum = running_sum * rescale + jnp.sum(weights, axis=2)
        product = jnp.einsum(
            "nqk,nkd->nqd",
            weights.astype(jnp.bfloat16),
            value_block,
            preferred_element_type=jnp.float32,
        )
        return (new_max, new_sum, accumulated * rescale[:, :, None] + product)

    return lax.fori_loop(0, key_count // block_len, one_block, partial_value)


def finish_state(partial_value):
    return (partial_value[2] / partial_value[1][:, :, None]).astype(jnp.bfloat16)[:, None]


def convolve(time_stack, conv_weight, conv_bias):
    row_count = time_stack.shape[3] - 2
    col_count = time_stack.shape[4]
    widened = jnp.pad(time_stack, ((0, 0), (0, 0), (0, 0), (0, 0), (1, 1)))
    shifted = []
    for t_shift in range(3):
        for y_shift in range(3):
            for x_shift in range(3):
                shifted.append(
                    widened[
                        :, t_shift, :, y_shift : y_shift + row_count, x_shift : x_shift + col_count
                    ]
                )
    columns = jnp.stack(shifted, axis=1).reshape(
        time_stack.shape[0], 27 * time_stack.shape[2], row_count * col_count
    )
    kernel = conv_weight.reshape(27 * time_stack.shape[2], conv_weight.shape[-1])
    result = (
        jnp.einsum("ko,bkp->bop", kernel, columns, preferred_element_type=jnp.float32)
        + conv_bias[None, :, None]
    )
    return result.astype(jnp.bfloat16)


def body(
    projections,
    residual,
    out_proj,
    modulation,
    final_weight,
    final_bias,
    noisy_latents,
    step_size,
    conv_weight,
    conv_bias,
):
    videos_here = projections.shape[1]
    tok_here = projections.shape[4]
    head_size = projections.shape[5]
    seq_count = lax.axis_size("seq")
    pair_major = projections.reshape(
        3, seq_count, videos_here * HEADS // seq_count, 1, tok_here, head_size
    )
    kv_frames = lax.all_gather(pair_major[1:], "blk", axis=3, tiled=True)
    received = (
        lax.all_to_all(pair_major[:1], "seq", split_axis=1, concat_axis=4, tiled=True),
        lax.all_to_all(kv_frames, "seq", split_axis=1, concat_axis=4, tiled=True),
    )
    queries = received[0][0, 0, :, 0]
    partial_value = attend_keys(
        initial_state(queries), queries, received[1][0, 0], received[1][1, 0]
    )
    attended = finish_state(partial_value)
    token_major = lax.all_to_all(attended, "seq", split_axis=2, concat_axis=0, tiled=True)
    token_major = token_major.reshape(videos_here, HEADS, 1, tok_here, head_size)
    width_all = HEADS * head_size
    token_rows = jnp.transpose(token_major, (0, 2, 3, 1, 4)).reshape(
        videos_here * tok_here, width_all
    )
    projected = jnp.dot(
        token_rows,
        lax.all_gather(out_proj, "blk", axis=0, tiled=True),
        preferred_element_type=jnp.float32,
    )
    projected = jnp.transpose(
        projected.reshape(videos_here, 1, tok_here, HEADS, head_size), (0, 3, 1, 2, 4)
    )
    factors = modulation.reshape(3, videos_here, HEADS, 1, 1, head_size)
    mixed = residual.astype(jnp.float32) + factors[2] * projected
    center = jnp.mean(mixed, axis=(1, 4), keepdims=True)
    spread = jnp.mean(jnp.square(mixed - center), axis=(1, 4), keepdims=True)
    normed = (mixed - center) * lax.rsqrt(spread + 1e-06)
    modulated = (normed * (1.0 + factors[1]) + factors[0]).astype(jnp.bfloat16)
    out_weight = final_weight.reshape(HEADS, head_size, final_weight.shape[1])
    prediction = (
        jnp.einsum("vhftd,hdo->vfto", modulated, out_weight, preferred_element_type=jnp.float32)
        + final_bias
    )
    latents = ((noisy_latents + step_size[:, None, None, None] * prediction) / 0.476986).astype(
        jnp.bfloat16
    )
    latent_image = latents.reshape(videos_here, 1, ROWS_DEV, PATCH_COLS, LATENT_CH, PATCH, PATCH)
    latent_image = jnp.transpose(latent_image, (0, 1, 4, 2, 5, 3, 6))
    latent_image = latent_image.reshape(
        videos_here, 1, LATENT_CH, PATCH * ROWS_DEV, PATCH * PATCH_COLS
    )
    tile_frames = lax.all_to_all(latent_image, "blk", split_axis=0, concat_axis=1, tiled=True)[0]
    extended = extended_2(tile_frames, (("seq", 2),), 1)
    padded = jnp.concatenate([extended[:1], extended[:1], extended], axis=0)
    frame_total = tile_frames.shape[0]
    time_stack = jnp.stack(
        [padded[0:frame_total], padded[1 : frame_total + 1], padded[2 : frame_total + 2]], axis=1
    )
    decoded = convolve(time_stack, conv_weight, conv_bias)[None]
    return decoded


def fits(mesh):
    return mesh.shape["seq"] == 2 and mesh.shape["blk"] == 4 and mesh.shape["prompt"] == 4


def dot(lhs, rhs, lhs_dim=1, rhs_dim=0):
    return lax.dot_general(
        lhs, rhs, (((lhs_dim,), (rhs_dim,)), ((), ())), preferred_element_type=jnp.float32
    )


def fused_kernel(
    proj,
    res_in,
    out_w,
    noisy_in,
    mod_in,
    final_in,
    final_b_in,
    conv_in,
    conv_b_in,
    step,
    out,
    qkv,
    res,
    noisy,
    rows,
    att,
    projected,
    centred,
    summary_out,
    summary_in,
    strip,
    spread,
    columns,
    bias,
    factors,
    mod,
    final_w,
    final_b,
    conv_w,
    conv_b,
    conv_t,
    qkv_send,
    qkv_recv,
    res_send,
    res_recv,
    noisy_send,
    noisy_recv,
    row_send,
    row_recv,
    forward_send,
    share_send,
    share_recv,
    att_send,
    att_recv,
    summary_sem,
    local_sem,
):
    p, s, b = lax.axis_index("prompt"), lax.axis_index("seq"), lax.axis_index("blk")
    other = 1 - s
    blks = [lax.rem(b + d, 4) for d in range(4)]
    froms = [lax.rem(b + 4 - d, 4) for d in range(4)]
    seqs = [s, other]
    prompts = [lax.rem(p + d, 4) for d in range(4)]
    prompt_froms = [lax.rem(p + 4 - d, 4) for d in range(4)]
    pairs = [(db, ds) for db in (2, 1, 3, 0) for ds in (0, 1) if (db, ds) != (0, 0)]

    barrier = pltpu.get_barrier_semaphore()
    for db, ds in pairs:
        pl.semaphore_signal(barrier, inc=1, device_id=(p, seqs[ds], blks[db]), device_id_type=pl.DeviceIdType.MESH)
    for dp in (1, 2, 3):
        pl.semaphore_signal(barrier, inc=1, device_id=(prompts[dp], s, b), device_id_type=pl.DeviceIdType.MESH)
    pl.semaphore_wait(barrier, 10)

    def remote(src, dst, send, recv, target):
        return pltpu.make_async_remote_copy(
            src_ref=src,
            dst_ref=dst,
            send_sem=send,
            recv_sem=recv,
            device_id=target,
            device_id_type=pl.DeviceIdType.MESH,
        )

    near = b + 1 - 2 * lax.rem(b, 2)
    inner = 2 - b // 2
    outer = 3 * (1 - b // 2)

    def row_slot(group, quarter):
        return rows.at[pl.ds(pl.multiple_of(group * 512 + quarter * 128, 128), 128)]

    def own_rows(quarter):
        return out_w.at[quarter, :, pl.ds(pl.multiple_of(s * 1024, 1024), 1024)]

    def row_copy(k, target, source):
        return remote(own_rows(p), row_slot(source, p), row_send.at[k], row_recv.at[source], (p, s, target))

    def forward_copy(k, source):
        slot = row_slot(source, p)
        return remote(slot, slot, forward_send.at[k], row_recv.at[source], (p, s, near))

    def share_copy(group, dp, source):
        return remote(
            row_slot(group, source),
            row_slot(group, source),
            share_send.at[group, dp],
            share_recv.at[group, source],
            (prompts[dp], s, b),
        )

    def qkv_copy(g, db, ds, frame, row):
        return remote(
            proj.at[:, blks[db], g, seqs[ds]],
            qkv.at[:, g, :, frame, row],
            qkv_send.at[g, db, ds],
            qkv_recv.at[g, frame, row],
            (p, seqs[ds], blks[db]),
        )

    def res_copy(db, ds, frame, row):
        return remote(
            res_in.at[blks[db], seqs[ds]],
            res.at[:, frame, row],
            res_send.at[db, ds],
            res_recv.at[frame, row],
            (p, seqs[ds], blks[db]),
        )

    def noisy_copy(db, ds, frame, row):
        return remote(
            noisy_in.at[blks[db]],
            noisy.at[frame, row],
            noisy_send.at[db, ds],
            noisy_recv.at[frame, row],
            (p, seqs[ds], blks[db]),
        )

    row_copy(0, inner, b).start()
    row_copy(1, near, b).start()
    for db, ds in pairs:
        qkv_copy(0, db, ds, b, s).start()
    own = [
        pltpu.make_async_copy(proj.at[:, b, g, s], qkv.at[:, g, :, b, s], local_sem.at[g]) for g in range(4)
    ]
    own.append(pltpu.make_async_copy(res_in.at[b, s], res.at[:, b, s], local_sem.at[4]))
    own.append(pltpu.make_async_copy(noisy_in.at[b], noisy.at[b, s], local_sem.at[5]))
    for quarter in range(4):
        own.append(pltpu.make_async_copy(own_rows(quarter), row_slot(b, quarter), local_sem.at[6 + quarter]))
    tables = ((mod_in, mod), (final_in, final_w), (final_b_in, final_b), (conv_in, conv_w), (conv_b_in, conv_b))
    for k, (src, dst) in enumerate(tables):
        own.append(pltpu.make_async_copy(src, dst, local_sem.at[10 + k]))
    for copy in own:
        copy.start()

    def share(source):
        for dp in (1, 2, 3):
            share_copy(source, dp, p).start()

    row_copy(0, near, near).wait_recv()
    share(near)

    @pl.when(lax.rem(b, 3) != 0)
    def _():
        for k, source in enumerate((inner, outer)):
            row_copy(0, near, source).wait_recv()
            forward_copy(k, source).start()
            share(source)

    for g in range(1, 4):
        for db, ds in pairs:
            qkv_copy(g, db, ds, b, s).start()
    for db, ds in pairs:
        noisy_copy(db, ds, b, s).start()
        res_copy(db, ds, b, s).start()

    for half in range(2):
        at_row = lax.broadcasted_iota(jnp.int32, (256, 768), 0)
        at_col = lax.broadcasted_iota(jnp.int32, (256, 768), 1)
        same = (at_row >> 6) == ((at_col >> 6) & 3)
        place = (at_col & 63) == 2 * (at_row & 31) + (half + 1) - (at_col >> 8)
        spread[half * 256 : half * 256 + 256, :] = jnp.where(same & place, 1.0, 0.0).astype(jnp.bfloat16)
    for copy in own[10:]:
        copy.wait()
    for k in range(3):
        video = lax.broadcasted_iota(jnp.int32, (4, 2048), 0)
        factors[k : k + 1, :] = jnp.sum(jnp.where(video == b, mod[k], 0.0), axis=0, keepdims=True)
    bias[...] = jnp.broadcast_to(conv_b[...], (128, 512)).T

    conv_t[...] = conv_w[...].T

    def split(value):
        high = value.astype(jnp.bfloat16)
        return high.astype(jnp.float32), value - high.astype(jnp.float32)

    row = lax.broadcasted_iota(jnp.int32, (8, 1024), 0)
    tilts = []
    moved = final_b[...]
    for half in range(2):
        lanes = slice(half * 1024, half * 1024 + 1024)
        high, low = split(1.0 + factors[1:2, lanes])
        shift_high, shift_low = split(factors[0:1, lanes])
        parts = jnp.where(row == 0, high, 0.0) + jnp.where(row == 1, low, 0.0)
        parts = parts + jnp.where(row == 2, shift_high, 0.0) + jnp.where(row == 3, shift_low, 0.0)
        sums = dot(parts.astype(jnp.bfloat16), final_w[:, lanes], 1, 1)
        tilts.append(sums[0:1] + sums[1:2])
        moved = moved + sums[2:3] + sums[3:4]
    tilt_mine = jnp.where(s == 0, tilts[0], tilts[1])
    tilt_other = jnp.where(s == 0, tilts[1], tilts[0])

    @pl.when(lax.rem(b, 3) == 0)
    def _():
        for source in (inner, outer):
            row_copy(0, near, source).wait_recv()
            share(source)

    def att_copy(g, side):
        cols = att.at[:, pl.ds(pl.multiple_of((4 * g + 2 * side) * 128, 256), 256)]
        return remote(cols, cols, att_send.at[g], att_recv.at[g], (p, other, b))

    scale = 128 ** (-0.5)
    for g in range(4):
        own[g].wait()
        for db, ds in pairs:
            qkv_copy(g, db, ds, froms[db], seqs[ds]).wait_recv()
        for k in range(2):
            q = qkv[0, g, k].reshape(256, 128)
            key = qkv[1, g, k].reshape(256, 128)
            value = qkv[2, g, k].reshape(256, 128)
            scores = dot(q, key, 1, 1) * scale
            weights = jnp.exp(scores - jnp.max(scores, axis=1, keepdims=True))
            totals = jnp.sum(weights, axis=1, keepdims=True)
            result = (dot(weights.astype(jnp.bfloat16), value) / totals).astype(jnp.bfloat16)
            att[:, pl.ds(pl.multiple_of((4 * g + 2 * s + k) * 128, 128), 128)] = result
        att_copy(g, s).start()
    for quarter in range(4):
        own[6 + quarter].wait()
    for source in (near, inner, outer):
        for dp in (1, 2, 3):
            share_copy(source, dp, prompt_froms[dp]).wait_recv()
    for done in range(4):
        att_copy(done, other).wait_recv()
    for n in range(2):
        lanes = slice(n * 512, n * 512 + 512)
        projected[:, lanes] = dot(att[...], rows[:, lanes])

    own[4].wait()
    for db, ds in pairs:
        res_copy(db, ds, froms[db], seqs[ds]).wait_recv()
    total = jnp.zeros((256, 128), jnp.float32)
    for h in range(8):
        lanes = slice(h * 128, h * 128 + 128)
        gate = jnp.where(s == 0, factors[2:3, lanes], factors[2:3, 1024 + h * 128 : 1152 + h * 128])
        value = res[h].reshape(256, 128).astype(jnp.float32) + gate * projected[:, lanes]
        projected[:, lanes] = value
        total = total + value
    center = jnp.sum(total, axis=1, keepdims=True) * (1.0 / 1024)
    total = jnp.zeros((256, 128), jnp.float32)
    for h in range(8):
        lanes = slice(h * 128, h * 128 + 128)
        away = projected[:, lanes] - center
        total = total + jnp.square(away)
        gain = jnp.where(s == 0, factors[1:2, lanes], factors[1:2, 1024 + h * 128 : 1152 + h * 128])
        centred[:, lanes] = (away * (1.0 + gain)).astype(jnp.bfloat16)
    squares = jnp.sum(total, axis=1, keepdims=True)
    weighted = dot(centred[...], final_w[:, pl.ds(pl.multiple_of(s * 1024, 1024), 1024)], 1, 1)
    summary_out[:, 0:64] = weighted
    lane = lax.broadcasted_iota(jnp.int32, (256, 64), 1)
    summary_out[:, 64:128] = jnp.where(lane == 0, center, jnp.where(lane == 1, squares, 0.0))
    summary = remote(summary_out, summary_in, summary_sem.at[0], summary_sem.at[1], (p, other, b))
    summary.start()
    own[5].wait()
    for db, ds in pairs:
        noisy_copy(db, ds, froms[db], seqs[ds]).wait_recv()
    start = noisy[...].reshape(256, 64)
    summary.wait_recv()
    center_other = summary_in[:, 64:65]
    squares = squares + summary_in[:, 65:66]
    apart = (center - center_other) * 0.5
    inverse = lax.rsqrt(squares * (1.0 / 2048) + jnp.square(apart) + 1e-06)
    weighted = weighted + summary_in[:, 0:64] + apart * (tilt_mine - tilt_other)
    prediction = inverse * weighted + moved
    latents = ((start + step[b] * prediction) / 0.476986).astype(jnp.bfloat16)

    to = lax.broadcasted_iota(jnp.int32, (64, 64), 0)
    channel = lax.broadcasted_iota(jnp.int32, (64, 64), 1)
    pick = jnp.where(channel == 4 * (to & 15) + (to >> 4), 1.0, 0.0).astype(jnp.bfloat16)
    image = dot(pick, latents, 1, 1)
    row_of = (lax.broadcasted_iota(jnp.int32, (16, 256), 1) >> 5) & 1
    for r in range(4):
        here = row_of == s + (r + 1) // 2 - 1
        for half in range(2):
            at = (1 - r % 2) * 32 + half * 16
            kept = jnp.where(here, image[at : at + 16], 0.0).astype(jnp.bfloat16)
            strip[r * 16 : r * 16 + 16, half * 256 : half * 256 + 256] = kept
    shifted = dot(strip[...], spread[...])
    for e in range(3):
        for f in range(4):
            lanes = slice(e * 256 + f * 64, e * 256 + f * 64 + 64)
            block = jnp.concatenate([shifted[0:48, lanes], shifted[16:64, lanes]], axis=1).astype(jnp.bfloat16)
            for t in range(3):
                for frame in range(4):
                    if max(frame + t - 2, 0) == f:
                        for y in range(3):
                            at = (t * 9 + y * 3 + e) * 16
                            columns[at : at + 16, frame * 128 : frame * 128 + 128] = block[y * 16 : y * 16 + 16]
    for f in range(4):
        decoded = dot(conv_t[...], columns[:, f * 128 : f * 128 + 128])
        out[f] = (decoded + bias[...]).astype(jnp.bfloat16)

    for k, source in enumerate((near, inner, outer)):
        if k < 2:
            row_copy(k, near, b).wait_send()
        else:

            @pl.when(lax.rem(b, 3) != 0)
            def _():
                forward_copy(0, inner).wait_send()
                forward_copy(1, outer).wait_send()

        for dp in (1, 2, 3):
            share_copy(source, dp, p).wait_send()
    for db, ds in pairs:
        res_copy(db, ds, b, s).wait_send()
        noisy_copy(db, ds, b, s).wait_send()
        for g in range(4):
            qkv_copy(g, db, ds, b, s).wait_send()
    for g in range(4):
        att_copy(g, s).wait_send()
    summary.wait_send()


def fused(
    projections,
    residual,
    out_proj,
    modulation,
    final_weight,
    final_bias,
    noisy_latents,
    step_size,
    conv_weight,
    conv_bias,
):
    anywhere = pl.BlockSpec(memory_space=pl.ANY)
    vmem = pl.BlockSpec(memory_space=pltpu.VMEM)
    smem = pl.BlockSpec(memory_space=pltpu.SMEM)
    half, full = jnp.bfloat16, jnp.float32
    dma = pltpu.SemaphoreType.DMA
    decoded = pl.pallas_call(
        fused_kernel,
        out_shape=jax.ShapeDtypeStruct((4, 512, 128), half),
        in_specs=[anywhere] * 9 + [smem],
        out_specs=vmem,
        scratch_shapes=[
            pltpu.VMEM((3, 4, 2, 4, 2, 32, 128), half),
            pltpu.VMEM((8, 4, 2, 32, 128), half),
            pltpu.VMEM((4, 2, 32, 64), full),
            pltpu.VMEM((2048, 1024), half),
            pltpu.VMEM((256, 2048), half),
            pltpu.VMEM((256, 1024), full),
            pltpu.VMEM((256, 1024), half),
            pltpu.VMEM((256, 128), full),
            pltpu.VMEM((256, 128), full),
            pltpu.VMEM((64, 512), half),
            pltpu.VMEM((512, 768), half),
            pltpu.VMEM((432, 512), half),
            pltpu.VMEM((512, 128), full),
            pltpu.VMEM((8, 2048), full),
            pltpu.VMEM((3, 4, 2048), full),
            pltpu.VMEM((64, 2048), half),
            pltpu.VMEM((1, 64), full),
            pltpu.VMEM((432, 512), half),
            pltpu.VMEM((1, 512), full),
            pltpu.VMEM((512, 432), half),
            dma((4, 4, 2)),
            dma((4, 4, 2)),
            dma((4, 2)),
            dma((4, 2)),
            dma((4, 2)),
            dma((4, 2)),
            dma((2,)),
            dma((4,)),
            dma((2,)),
            dma((4, 4)),
            dma((4, 4)),
            dma((4,)),
            dma((4,)),
            dma((2,)),
            dma((15,)),
        ],
        compiler_params=pltpu.CompilerParams(
            collective_id=0, has_side_effects=True, vmem_limit_bytes=60 * 1024 * 1024
        ),
    )(
        projections.reshape(3, 4, 4, 2, 2, 32, 128),
        residual.reshape(4, 2, 8, 32, 128),
        out_proj.reshape(4, 128, 2048),
        noisy_latents.reshape(4, 32, 64),
        modulation,
        final_weight.T,
        final_bias.reshape(1, 64),
        conv_weight.reshape(432, 512),
        conv_bias.reshape(1, 512),
        step_size,
    )
    return decoded[None]


def solution(mesh):
    return jax.shard_map(
        fused if fits(mesh) else body,
        mesh=mesh,
        in_specs=(
            P(None, None, None, "blk", "seq", None),
            P(None, None, "blk", "seq", None),
            P("blk", None),
            P(),
            P(),
            P(),
            P(None, "blk", "seq", None),
            P(),
            P(),
            P(),
        ),
        out_specs=P(("prompt", "blk"), None, None, "seq"),
        check_vma=False,
    )
```

```python
import functools
import math

import jax
import jax.numpy as jnp
from jax import lax
from jax.experimental import pallas as pl
from jax.experimental.pallas import tpu as pltpu
from jax.sharding import PartitionSpec as P

HEADS = 16
LATENT_CH = 16
PATCH = 2
ROWS_DEV = 1
PATCH_COLS = 32


def extended_2(cells, sides, width):
    for axis, dim in sides:
        count = lax.axis_size(axis)
        ends = count - 1
        head = lax.slice_in_dim(cells, 0, width, axis=dim)
        tail = lax.slice_in_dim(cells, cells.shape[dim] - width, cells.shape[dim], axis=dim)
        cells = jnp.concatenate(
            [
                lax.ppermute(tail, axis, [(i, (i + 1) % count) for i in range(ends)]),
                cells,
                lax.ppermute(head, axis, [((i + 1) % count, i) for i in range(ends)]),
            ],
            axis=dim,
        )
    return cells


def initial_state(queries):
    rows_shape = queries.shape[:2]
    return (
        jnp.full(rows_shape, -jnp.inf, jnp.float32),
        jnp.zeros(rows_shape, jnp.float32),
        jnp.zeros(queries.shape, jnp.float32),
    )


def attend_keys(partial_value, queries, key_part, value_part):
    key_rows = key_part.reshape(key_part.shape[0], -1, key_part.shape[-1])
    value_rows = value_part.reshape(value_part.shape[0], -1, value_part.shape[-1])
    key_count = key_rows.shape[1]
    block_len = math.gcd(key_count, 512)
    scale_factor = queries.shape[-1] ** (-0.5)

    def one_block(offset, state):
        running_max, running_sum, accumulated = state
        key_block = lax.dynamic_slice_in_dim(key_rows, offset * block_len, block_len, 1)
        value_block = lax.dynamic_slice_in_dim(value_rows, offset * block_len, block_len, 1)
        scores = (
            jnp.einsum("nqd,nkd->nqk", queries, key_block, preferred_element_type=jnp.float32)
            * scale_factor
        )
        new_max = jnp.maximum(running_max, jnp.max(scores, axis=2))
        rescale = jnp.exp(running_max - new_max)
        weights = jnp.exp(scores - new_max[:, :, None])
        new_sum = running_sum * rescale + jnp.sum(weights, axis=2)
        product = jnp.einsum(
            "nqk,nkd->nqd",
            weights.astype(jnp.bfloat16),
            value_block,
            preferred_element_type=jnp.float32,
        )
        return (new_max, new_sum, accumulated * rescale[:, :, None] + product)

    return lax.fori_loop(0, key_count // block_len, one_block, partial_value)


def finish_state(partial_value):
    return (partial_value[2] / partial_value[1][:, :, None]).astype(jnp.bfloat16)[:, None]


def convolve(time_stack, conv_weight, conv_bias):
    row_count = time_stack.shape[3] - 2
    col_count = time_stack.shape[4]
    widened = jnp.pad(time_stack, ((0, 0), (0, 0), (0, 0), (0, 0), (1, 1)))
    shifted = []
    for t_shift in range(3):
        for y_shift in range(3):
            for x_shift in range(3):
                shifted.append(
                    widened[
                        :, t_shift, :, y_shift : y_shift + row_count, x_shift : x_shift + col_count
                    ]
                )
    columns = jnp.stack(shifted, axis=1).reshape(
        time_stack.shape[0], 27 * time_stack.shape[2], row_count * col_count
    )
    kernel = conv_weight.reshape(27 * time_stack.shape[2], conv_weight.shape[-1])
    result = (
        jnp.einsum("ko,bkp->bop", kernel, columns, preferred_element_type=jnp.float32)
        + conv_bias[None, :, None]
    )
    return result.astype(jnp.bfloat16)


def body(
    projections,
    residual,
    out_proj,
    modulation,
    final_weight,
    final_bias,
    noisy_latents,
    step_size,
    conv_weight,
    conv_bias,
):
    videos_here = projections.shape[1]
    tok_here = projections.shape[4]
    head_size = projections.shape[5]
    seq_count = lax.axis_size("seq")
    pair_major = projections.reshape(
        3, seq_count, videos_here * HEADS // seq_count, 1, tok_here, head_size
    )
    kv_frames = lax.all_gather(pair_major[1:], "blk", axis=3, tiled=True)
    received = (
        lax.all_to_all(pair_major[:1], "seq", split_axis=1, concat_axis=4, tiled=True),
        lax.all_to_all(kv_frames, "seq", split_axis=1, concat_axis=4, tiled=True),
    )
    queries = received[0][0, 0, :, 0]
    partial_value = attend_keys(
        initial_state(queries), queries, received[1][0, 0], received[1][1, 0]
    )
    attended = finish_state(partial_value)
    token_major = lax.all_to_all(attended, "seq", split_axis=2, concat_axis=0, tiled=True)
    token_major = token_major.reshape(videos_here, HEADS, 1, tok_here, head_size)
    width_all = HEADS * head_size
    token_rows = jnp.transpose(token_major, (0, 2, 3, 1, 4)).reshape(
        videos_here * tok_here, width_all
    )
    projected = jnp.dot(
        token_rows,
        lax.all_gather(out_proj, "blk", axis=0, tiled=True),
        preferred_element_type=jnp.float32,
    )
    projected = jnp.transpose(
        projected.reshape(videos_here, 1, tok_here, HEADS, head_size), (0, 3, 1, 2, 4)
    )
    factors = modulation.reshape(3, videos_here, HEADS, 1, 1, head_size)
    mixed = residual.astype(jnp.float32) + factors[2] * projected
    center = jnp.mean(mixed, axis=(1, 4), keepdims=True)
    spread = jnp.mean(jnp.square(mixed - center), axis=(1, 4), keepdims=True)
    normed = (mixed - center) * lax.rsqrt(spread + 1e-06)
    modulated = (normed * (1.0 + factors[1]) + factors[0]).astype(jnp.bfloat16)
    out_weight = final_weight.reshape(HEADS, head_size, final_weight.shape[1])
    prediction = (
        jnp.einsum("vhftd,hdo->vfto", modulated, out_weight, preferred_element_type=jnp.float32)
        + final_bias
    )
    latents = ((noisy_latents + step_size[:, None, None, None] * prediction) / 0.476986).astype(
        jnp.bfloat16
    )
    latent_image = latents.reshape(videos_here, 1, ROWS_DEV, PATCH_COLS, LATENT_CH, PATCH, PATCH)
    latent_image = jnp.transpose(latent_image, (0, 1, 4, 2, 5, 3, 6))
    latent_image = latent_image.reshape(
        videos_here, 1, LATENT_CH, PATCH * ROWS_DEV, PATCH * PATCH_COLS
    )
    tile_frames = lax.all_to_all(latent_image, "blk", split_axis=0, concat_axis=1, tiled=True)[0]
    extended = extended_2(tile_frames, (("seq", 2),), 1)
    padded = jnp.concatenate([extended[:1], extended[:1], extended], axis=0)
    frame_total = tile_frames.shape[0]
    time_stack = jnp.stack(
        [padded[0:frame_total], padded[1 : frame_total + 1], padded[2 : frame_total + 2]], axis=1
    )
    decoded = convolve(time_stack, conv_weight, conv_bias)[None]
    return decoded


def fits(mesh):
    return mesh.shape["seq"] == 2 and mesh.shape["blk"] == 4 and mesh.shape["prompt"] == 4


def dot(lhs, rhs, lhs_dim=1, rhs_dim=0):
    return lax.dot_general(
        lhs, rhs, (((lhs_dim,), (rhs_dim,)), ((), ())), preferred_element_type=jnp.float32
    )


def fused_kernel(
    proj,
    res_in,
    out_w,
    noisy_in,
    mod_in,
    final_in,
    final_b_in,
    conv_in,
    conv_b_in,
    step,
    out,
    qkv,
    res,
    noisy,
    rows,
    att,
    projected,
    centred,
    summary_out,
    summary_in,
    strip,
    spread,
    columns,
    bias,
    factors,
    mod,
    final_w,
    final_b,
    conv_w,
    conv_b,
    conv_t,
    qkv_send,
    qkv_recv,
    res_send,
    res_recv,
    noisy_send,
    noisy_recv,
    row_send,
    row_recv,
    forward_send,
    share_send,
    share_recv,
    att_send,
    att_recv,
    summary_sem,
    local_sem,
):
    p, s, b = lax.axis_index("prompt"), lax.axis_index("seq"), lax.axis_index("blk")
    other = 1 - s
    blks = [lax.rem(b + d, 4) for d in range(4)]
    froms = [lax.rem(b + 4 - d, 4) for d in range(4)]
    seqs = [s, other]
    prompts = [lax.rem(p + d, 4) for d in range(4)]
    prompt_froms = [lax.rem(p + 4 - d, 4) for d in range(4)]
    pairs = [(db, ds) for db in (2, 1, 3, 0) for ds in (0, 1) if (db, ds) != (0, 0)]

    barrier = pltpu.get_barrier_semaphore()
    for db, ds in pairs:
        pl.semaphore_signal(barrier, inc=1, device_id=(p, seqs[ds], blks[db]), device_id_type=pl.DeviceIdType.MESH)
    for dp in (1, 2, 3):
        pl.semaphore_signal(barrier, inc=1, device_id=(prompts[dp], s, b), device_id_type=pl.DeviceIdType.MESH)
    pl.semaphore_wait(barrier, 10)

    def remote(src, dst, send, recv, target):
        return pltpu.make_async_remote_copy(
            src_ref=src,
            dst_ref=dst,
            send_sem=send,
            recv_sem=recv,
            device_id=target,
            device_id_type=pl.DeviceIdType.MESH,
        )

    near = b + 1 - 2 * lax.rem(b, 2)
    inner = 2 - b // 2
    outer = 3 * (1 - b // 2)

    def row_slot(group, quarter):
        return rows.at[pl.ds(pl.multiple_of(group * 512 + quarter * 128, 128), 128)]

    def own_rows(quarter):
        return out_w.at[quarter, :, pl.ds(pl.multiple_of(s * 1024, 1024), 1024)]

    def row_copy(k, target, source):
        return remote(own_rows(p), row_slot(source, p), row_send.at[k], row_recv.at[source], (p, s, target))

    def forward_copy(k, source):
        slot = row_slot(source, p)
        return remote(slot, slot, forward_send.at[k], row_recv.at[source], (p, s, near))

    def share_copy(group, dp, source):
        return remote(
            row_slot(group, source),
            row_slot(group, source),
            share_send.at[group, dp],
            share_recv.at[group, source],
            (prompts[dp], s, b),
        )

    def qkv_copy(g, db, ds, frame, row):
        return remote(
            proj.at[:, blks[db], g, seqs[ds]],
            qkv.at[:, g, :, frame, row],
            qkv_send.at[g, db, ds],
            qkv_recv.at[g, frame, row],
            (p, seqs[ds], blks[db]),
        )

    def res_copy(db, ds, frame, row):
        return remote(
            res_in.at[blks[db], seqs[ds]],
            res.at[:, frame, row],
            res_send.at[db, ds],
            res_recv.at[frame, row],
            (p, seqs[ds], blks[db]),
        )

    def noisy_copy(db, ds, frame, row):
        return remote(
            noisy_in.at[blks[db]],
            noisy.at[frame, row],
            noisy_send.at[db, ds],
            noisy_recv.at[frame, row],
            (p, seqs[ds], blks[db]),
        )

    row_copy(0, inner, b).start()
    row_copy(1, near, b).start()
    for g in range(2):
        for db, ds in pairs:
            qkv_copy(g, db, ds, b, s).start()
    own = [
        pltpu.make_async_copy(proj.at[:, b, g, s], qkv.at[:, g, :, b, s], local_sem.at[g]) for g in range(4)
    ]
    own.append(pltpu.make_async_copy(res_in.at[b, s], res.at[:, b, s], local_sem.at[4]))
    own.append(pltpu.make_async_copy(noisy_in.at[b], noisy.at[b, s], local_sem.at[5]))
    for quarter in range(4):
        own.append(pltpu.make_async_copy(own_rows(quarter), row_slot(b, quarter), local_sem.at[6 + quarter]))
    tables = ((mod_in, mod), (final_in, final_w), (final_b_in, final_b), (conv_in, conv_w), (conv_b_in, conv_b))
    for k, (src, dst) in enumerate(tables):
        own.append(pltpu.make_async_copy(src, dst, local_sem.at[10 + k]))
    for copy in own:
        copy.start()

    def share(source):
        for dp in (1, 2, 3):
            share_copy(source, dp, p).start()

    row_copy(0, near, near).wait_recv()
    share(near)

    @pl.when(lax.rem(b, 3) != 0)
    def _():
        for k, source in enumerate((inner, outer)):
            row_copy(0, near, source).wait_recv()
            forward_copy(k, source).start()
            share(source)

    for g in range(2, 4):
        for db, ds in pairs:
            qkv_copy(g, db, ds, b, s).start()
    for db, ds in pairs:
        noisy_copy(db, ds, b, s).start()
        res_copy(db, ds, b, s).start()

    for half in range(2):
        at_row = lax.broadcasted_iota(jnp.int32, (256, 768), 0)
        at_col = lax.broadcasted_iota(jnp.int32, (256, 768), 1)
        same = (at_row >> 6) == ((at_col >> 6) & 3)
        place = (at_col & 63) == 2 * (at_row & 31) + (half + 1) - (at_col >> 8)
        spread[half * 256 : half * 256 + 256, :] = jnp.where(same & place, 1.0, 0.0).astype(jnp.bfloat16)
    for copy in own[10:]:
        copy.wait()
    for k in range(3):
        video = lax.broadcasted_iota(jnp.int32, (4, 2048), 0)
        factors[k : k + 1, :] = jnp.sum(jnp.where(video == b, mod[k], 0.0), axis=0, keepdims=True)
    bias[...] = jnp.broadcast_to(conv_b[...], (128, 512)).T

    conv_t[...] = conv_w[...].T

    def split(value):
        high = value.astype(jnp.bfloat16)
        return high.astype(jnp.float32), value - high.astype(jnp.float32)

    row = lax.broadcasted_iota(jnp.int32, (8, 1024), 0)
    tilts = []
    moved = final_b[...]
    for half in range(2):
        lanes = slice(half * 1024, half * 1024 + 1024)
        high, low = split(1.0 + factors[1:2, lanes])
        shift_high, shift_low = split(factors[0:1, lanes])
        parts = jnp.where(row == 0, high, 0.0) + jnp.where(row == 1, low, 0.0)
        parts = parts + jnp.where(row == 2, shift_high, 0.0) + jnp.where(row == 3, shift_low, 0.0)
        sums = dot(parts.astype(jnp.bfloat16), final_w[:, lanes], 1, 1)
        tilts.append(sums[0:1] + sums[1:2])
        moved = moved + sums[2:3] + sums[3:4]
    tilt_mine = jnp.where(s == 0, tilts[0], tilts[1])
    tilt_other = jnp.where(s == 0, tilts[1], tilts[0])

    @pl.when(lax.rem(b, 3) == 0)
    def _():
        for source in (inner, outer):
            row_copy(0, near, source).wait_recv()
            share(source)

    def att_copy(g, side):
        cols = att.at[:, pl.ds(pl.multiple_of((4 * g + 2 * side) * 128, 256), 256)]
        return remote(cols, cols, att_send.at[g], att_recv.at[g], (p, other, b))

    scale = 128 ** (-0.5)
    for g in range(4):
        own[g].wait()
        for db, ds in pairs:
            qkv_copy(g, db, ds, froms[db], seqs[ds]).wait_recv()
        for k in range(2):
            q = qkv[0, g, k].reshape(256, 128)
            key = qkv[1, g, k].reshape(256, 128)
            value = qkv[2, g, k].reshape(256, 128)
            scores = dot(q, key, 1, 1) * scale
            weights = jnp.exp(scores - jnp.max(scores, axis=1, keepdims=True))
            totals = jnp.sum(weights, axis=1, keepdims=True)
            result = (dot(weights.astype(jnp.bfloat16), value) / totals).astype(jnp.bfloat16)
            att[:, pl.ds(pl.multiple_of((4 * g + 2 * s + k) * 128, 128), 128)] = result
        att_copy(g, s).start()
    for quarter in range(4):
        own[6 + quarter].wait()
    for source in (near, inner, outer):
        for dp in (1, 2, 3):
            share_copy(source, dp, prompt_froms[dp]).wait_recv()
    for done in range(4):
        att_copy(done, other).wait_recv()
    for n in range(2):
        lanes = slice(n * 512, n * 512 + 512)
        projected[:, lanes] = dot(att[...], rows[:, lanes])

    own[4].wait()
    for db, ds in pairs:
        res_copy(db, ds, froms[db], seqs[ds]).wait_recv()
    total = jnp.zeros((256, 128), jnp.float32)
    for h in range(8):
        lanes = slice(h * 128, h * 128 + 128)
        gate = jnp.where(s == 0, factors[2:3, lanes], factors[2:3, 1024 + h * 128 : 1152 + h * 128])
        value = res[h].reshape(256, 128).astype(jnp.float32) + gate * projected[:, lanes]
        projected[:, lanes] = value
        total = total + value
    center = jnp.sum(total, axis=1, keepdims=True) * (1.0 / 1024)
    total = jnp.zeros((256, 128), jnp.float32)
    for h in range(8):
        lanes = slice(h * 128, h * 128 + 128)
        away = projected[:, lanes] - center
        total = total + jnp.square(away)
        gain = jnp.where(s == 0, factors[1:2, lanes], factors[1:2, 1024 + h * 128 : 1152 + h * 128])
        centred[:, lanes] = (away * (1.0 + gain)).astype(jnp.bfloat16)
    squares = jnp.sum(total, axis=1, keepdims=True)
    weighted = dot(centred[...], final_w[:, pl.ds(pl.multiple_of(s * 1024, 1024), 1024)], 1, 1)
    summary_out[:, 0:64] = weighted
    lane = lax.broadcasted_iota(jnp.int32, (256, 64), 1)
    summary_out[:, 64:128] = jnp.where(lane == 0, center, jnp.where(lane == 1, squares, 0.0))
    summary = remote(summary_out, summary_in, summary_sem.at[0], summary_sem.at[1], (p, other, b))
    summary.start()
    own[5].wait()
    for db, ds in pairs:
        noisy_copy(db, ds, froms[db], seqs[ds]).wait_recv()
    start = noisy[...].reshape(256, 64)
    summary.wait_recv()
    center_other = summary_in[:, 64:65]
    squares = squares + summary_in[:, 65:66]
    apart = (center - center_other) * 0.5
    inverse = lax.rsqrt(squares * (1.0 / 2048) + jnp.square(apart) + 1e-06)
    weighted = weighted + summary_in[:, 0:64] + apart * (tilt_mine - tilt_other)
    prediction = inverse * weighted + moved
    latents = ((start + step[b] * prediction) / 0.476986).astype(jnp.bfloat16)

    to = lax.broadcasted_iota(jnp.int32, (64, 64), 0)
    channel = lax.broadcasted_iota(jnp.int32, (64, 64), 1)
    pick = jnp.where(channel == 4 * (to & 15) + (to >> 4), 1.0, 0.0).astype(jnp.bfloat16)
    image = dot(pick, latents, 1, 1)
    row_of = (lax.broadcasted_iota(jnp.int32, (16, 256), 1) >> 5) & 1
    for r in range(4):
        here = row_of == s + (r + 1) // 2 - 1
        for half in range(2):
            at = (1 - r % 2) * 32 + half * 16
            kept = jnp.where(here, image[at : at + 16], 0.0).astype(jnp.bfloat16)
            strip[r * 16 : r * 16 + 16, half * 256 : half * 256 + 256] = kept
    shifted = dot(strip[...], spread[...])
    for e in range(3):
        for f in range(4):
            lanes = slice(e * 256 + f * 64, e * 256 + f * 64 + 64)
            block = jnp.concatenate([shifted[0:48, lanes], shifted[16:64, lanes]], axis=1).astype(jnp.bfloat16)
            for t in range(3):
                for frame in range(4):
                    if max(frame + t - 2, 0) == f:
                        for y in range(3):
                            at = (t * 9 + y * 3 + e) * 16
                            columns[at : at + 16, frame * 128 : frame * 128 + 128] = block[y * 16 : y * 16 + 16]
    for f in range(4):
        decoded = dot(conv_t[...], columns[:, f * 128 : f * 128 + 128])
        out[f] = (decoded + bias[...]).astype(jnp.bfloat16)

    for k, source in enumerate((near, inner, outer)):
        if k < 2:
            row_copy(k, near, b).wait_send()
        else:

            @pl.when(lax.rem(b, 3) != 0)
            def _():
                forward_copy(0, inner).wait_send()
                forward_copy(1, outer).wait_send()

        for dp in (1, 2, 3):
            share_copy(source, dp, p).wait_send()
    for db, ds in pairs:
        res_copy(db, ds, b, s).wait_send()
        noisy_copy(db, ds, b, s).wait_send()
        for g in range(4):
            qkv_copy(g, db, ds, b, s).wait_send()
    for g in range(4):
        att_copy(g, s).wait_send()
    summary.wait_send()


def fused(
    projections,
    residual,
    out_proj,
    modulation,
    final_weight,
    final_bias,
    noisy_latents,
    step_size,
    conv_weight,
    conv_bias,
):
    anywhere = pl.BlockSpec(memory_space=pl.ANY)
    vmem = pl.BlockSpec(memory_space=pltpu.VMEM)
    smem = pl.BlockSpec(memory_space=pltpu.SMEM)
    half, full = jnp.bfloat16, jnp.float32
    dma = pltpu.SemaphoreType.DMA
    decoded = pl.pallas_call(
        fused_kernel,
        out_shape=jax.ShapeDtypeStruct((4, 512, 128), half),
        in_specs=[anywhere] * 9 + [smem],
        out_specs=vmem,
        scratch_shapes=[
            pltpu.VMEM((3, 4, 2, 4, 2, 32, 128), half),
            pltpu.VMEM((8, 4, 2, 32, 128), half),
            pltpu.VMEM((4, 2, 32, 64), full),
            pltpu.VMEM((2048, 1024), half),
            pltpu.VMEM((256, 2048), half),
            pltpu.VMEM((256, 1024), full),
            pltpu.VMEM((256, 1024), half),
            pltpu.VMEM((256, 128), full),
            pltpu.VMEM((256, 128), full),
            pltpu.VMEM((64, 512), half),
            pltpu.VMEM((512, 768), half),
            pltpu.VMEM((432, 512), half),
            pltpu.VMEM((512, 128), full),
            pltpu.VMEM((8, 2048), full),
            pltpu.VMEM((3, 4, 2048), full),
            pltpu.VMEM((64, 2048), half),
            pltpu.VMEM((1, 64), full),
            pltpu.VMEM((432, 512), half),
            pltpu.VMEM((1, 512), full),
            pltpu.VMEM((512, 432), half),
            dma((4, 4, 2)),
            dma((4, 4, 2)),
            dma((4, 2)),
            dma((4, 2)),
            dma((4, 2)),
            dma((4, 2)),
            dma((2,)),
            dma((4,)),
            dma((2,)),
            dma((4, 4)),
            dma((4, 4)),
            dma((4,)),
            dma((4,)),
            dma((2,)),
            dma((15,)),
        ],
        compiler_params=pltpu.CompilerParams(
            collective_id=0, has_side_effects=True, vmem_limit_bytes=60 * 1024 * 1024
        ),
    )(
        projections.reshape(3, 4, 4, 2, 2, 32, 128),
        residual.reshape(4, 2, 8, 32, 128),
        out_proj.reshape(4, 128, 2048),
        noisy_latents.reshape(4, 32, 64),
        modulation,
        final_weight.T,
        final_bias.reshape(1, 64),
        conv_weight.reshape(432, 512),
        conv_bias.reshape(1, 512),
        step_size,
    )
    return decoded[None]


def solution(mesh):
    return jax.shard_map(
        fused if fits(mesh) else body,
        mesh=mesh,
        in_specs=(
            P(None, None, None, "blk", "seq", None),
            P(None, None, "blk", "seq", None),
            P("blk", None),
            P(),
            P(),
            P(),
            P(None, "blk", "seq", None),
            P(),
            P(),
            P(),
        ),
        out_specs=P(("prompt", "blk"), None, None, "seq"),
        check_vma=False,
    )
```

```python
import functools
import math

import jax
import jax.numpy as jnp
from jax import lax
from jax.experimental import pallas as pl
from jax.experimental.pallas import tpu as pltpu
from jax.sharding import PartitionSpec as P

HEADS = 16
LATENT_CH = 16
PATCH = 2
ROWS_DEV = 1
PATCH_COLS = 32


def extended_2(cells, sides, width):
    for axis, dim in sides:
        count = lax.axis_size(axis)
        ends = count - 1
        head = lax.slice_in_dim(cells, 0, width, axis=dim)
        tail = lax.slice_in_dim(cells, cells.shape[dim] - width, cells.shape[dim], axis=dim)
        cells = jnp.concatenate(
            [
                lax.ppermute(tail, axis, [(i, (i + 1) % count) for i in range(ends)]),
                cells,
                lax.ppermute(head, axis, [((i + 1) % count, i) for i in range(ends)]),
            ],
            axis=dim,
        )
    return cells


def initial_state(queries):
    rows_shape = queries.shape[:2]
    return (
        jnp.full(rows_shape, -jnp.inf, jnp.float32),
        jnp.zeros(rows_shape, jnp.float32),
        jnp.zeros(queries.shape, jnp.float32),
    )


def attend_keys(partial_value, queries, key_part, value_part):
    key_rows = key_part.reshape(key_part.shape[0], -1, key_part.shape[-1])
    value_rows = value_part.reshape(value_part.shape[0], -1, value_part.shape[-1])
    key_count = key_rows.shape[1]
    block_len = math.gcd(key_count, 512)
    scale_factor = queries.shape[-1] ** (-0.5)

    def one_block(offset, state):
        running_max, running_sum, accumulated = state
        key_block = lax.dynamic_slice_in_dim(key_rows, offset * block_len, block_len, 1)
        value_block = lax.dynamic_slice_in_dim(value_rows, offset * block_len, block_len, 1)
        scores = (
            jnp.einsum("nqd,nkd->nqk", queries, key_block, preferred_element_type=jnp.float32)
            * scale_factor
        )
        new_max = jnp.maximum(running_max, jnp.max(scores, axis=2))
        rescale = jnp.exp(running_max - new_max)
        weights = jnp.exp(scores - new_max[:, :, None])
        new_sum = running_sum * rescale + jnp.sum(weights, axis=2)
        product = jnp.einsum(
            "nqk,nkd->nqd",
            weights.astype(jnp.bfloat16),
            value_block,
            preferred_element_type=jnp.float32,
        )
        return (new_max, new_sum, accumulated * rescale[:, :, None] + product)

    return lax.fori_loop(0, key_count // block_len, one_block, partial_value)


def finish_state(partial_value):
    return (partial_value[2] / partial_value[1][:, :, None]).astype(jnp.bfloat16)[:, None]


def convolve(time_stack, conv_weight, conv_bias):
    row_count = time_stack.shape[3] - 2
    col_count = time_stack.shape[4]
    widened = jnp.pad(time_stack, ((0, 0), (0, 0), (0, 0), (0, 0), (1, 1)))
    shifted = []
    for t_shift in range(3):
        for y_shift in range(3):
            for x_shift in range(3):
                shifted.append(
                    widened[
                        :, t_shift, :, y_shift : y_shift + row_count, x_shift : x_shift + col_count
                    ]
                )
    columns = jnp.stack(shifted, axis=1).reshape(
        time_stack.shape[0], 27 * time_stack.shape[2], row_count * col_count
    )
    kernel = conv_weight.reshape(27 * time_stack.shape[2], conv_weight.shape[-1])
    result = (
        jnp.einsum("ko,bkp->bop", kernel, columns, preferred_element_type=jnp.float32)
        + conv_bias[None, :, None]
    )
    return result.astype(jnp.bfloat16)


def body(
    projections,
    residual,
    out_proj,
    modulation,
    final_weight,
    final_bias,
    noisy_latents,
    step_size,
    conv_weight,
    conv_bias,
):
    videos_here = projections.shape[1]
    tok_here = projections.shape[4]
    head_size = projections.shape[5]
    seq_count = lax.axis_size("seq")
    pair_major = projections.reshape(
        3, seq_count, videos_here * HEADS // seq_count, 1, tok_here, head_size
    )
    kv_frames = lax.all_gather(pair_major[1:], "blk", axis=3, tiled=True)
    received = (
        lax.all_to_all(pair_major[:1], "seq", split_axis=1, concat_axis=4, tiled=True),
        lax.all_to_all(kv_frames, "seq", split_axis=1, concat_axis=4, tiled=True),
    )
    queries = received[0][0, 0, :, 0]
    partial_value = attend_keys(
        initial_state(queries), queries, received[1][0, 0], received[1][1, 0]
    )
    attended = finish_state(partial_value)
    token_major = lax.all_to_all(attended, "seq", split_axis=2, concat_axis=0, tiled=True)
    token_major = token_major.reshape(videos_here, HEADS, 1, tok_here, head_size)
    width_all = HEADS * head_size
    token_rows = jnp.transpose(token_major, (0, 2, 3, 1, 4)).reshape(
        videos_here * tok_here, width_all
    )
    projected = jnp.dot(
        token_rows,
        lax.all_gather(out_proj, "blk", axis=0, tiled=True),
        preferred_element_type=jnp.float32,
    )
    projected = jnp.transpose(
        projected.reshape(videos_here, 1, tok_here, HEADS, head_size), (0, 3, 1, 2, 4)
    )
    factors = modulation.reshape(3, videos_here, HEADS, 1, 1, head_size)
    mixed = residual.astype(jnp.float32) + factors[2] * projected
    center = jnp.mean(mixed, axis=(1, 4), keepdims=True)
    spread = jnp.mean(jnp.square(mixed - center), axis=(1, 4), keepdims=True)
    normed = (mixed - center) * lax.rsqrt(spread + 1e-06)
    modulated = (normed * (1.0 + factors[1]) + factors[0]).astype(jnp.bfloat16)
    out_weight = final_weight.reshape(HEADS, head_size, final_weight.shape[1])
    prediction = (
        jnp.einsum("vhftd,hdo->vfto", modulated, out_weight, preferred_element_type=jnp.float32)
        + final_bias
    )
    latents = ((noisy_latents + step_size[:, None, None, None] * prediction) / 0.476986).astype(
        jnp.bfloat16
    )
    latent_image = latents.reshape(videos_here, 1, ROWS_DEV, PATCH_COLS, LATENT_CH, PATCH, PATCH)
    latent_image = jnp.transpose(latent_image, (0, 1, 4, 2, 5, 3, 6))
    latent_image = latent_image.reshape(
        videos_here, 1, LATENT_CH, PATCH * ROWS_DEV, PATCH * PATCH_COLS
    )
    tile_frames = lax.all_to_all(latent_image, "blk", split_axis=0, concat_axis=1, tiled=True)[0]
    extended = extended_2(tile_frames, (("seq", 2),), 1)
    padded = jnp.concatenate([extended[:1], extended[:1], extended], axis=0)
    frame_total = tile_frames.shape[0]
    time_stack = jnp.stack(
        [padded[0:frame_total], padded[1 : frame_total + 1], padded[2 : frame_total + 2]], axis=1
    )
    decoded = convolve(time_stack, conv_weight, conv_bias)[None]
    return decoded


def fits(mesh):
    return mesh.shape["seq"] == 2 and mesh.shape["blk"] == 4 and mesh.shape["prompt"] == 4


def dot(lhs, rhs, lhs_dim=1, rhs_dim=0):
    return lax.dot_general(
        lhs, rhs, (((lhs_dim,), (rhs_dim,)), ((), ())), preferred_element_type=jnp.float32
    )


def fused_kernel(
    proj,
    res_in,
    out_w,
    noisy_in,
    mod_in,
    final_in,
    final_b_in,
    conv_in,
    conv_b_in,
    step,
    out,
    qkv,
    res,
    noisy,
    rows,
    att,
    projected,
    centred,
    summary_out,
    summary_in,
    strip,
    spread,
    columns,
    bias,
    factors,
    mod,
    final_w,
    final_b,
    conv_w,
    conv_b,
    conv_t,
    qkv_send,
    qkv_recv,
    res_send,
    res_recv,
    noisy_send,
    noisy_recv,
    row_send,
    row_recv,
    forward_send,
    share_send,
    share_recv,
    att_send,
    att_recv,
    summary_sem,
    local_sem,
):
    p, s, b = lax.axis_index("prompt"), lax.axis_index("seq"), lax.axis_index("blk")
    other = 1 - s
    blks = [lax.rem(b + d, 4) for d in range(4)]
    froms = [lax.rem(b + 4 - d, 4) for d in range(4)]
    seqs = [s, other]
    prompts = [lax.rem(p + d, 4) for d in range(4)]
    prompt_froms = [lax.rem(p + 4 - d, 4) for d in range(4)]
    pairs = [(db, ds) for db in (2, 1, 3, 0) for ds in (0, 1) if (db, ds) != (0, 0)]

    barrier = pltpu.get_barrier_semaphore()
    for db, ds in pairs:
        pl.semaphore_signal(barrier, inc=1, device_id=(p, seqs[ds], blks[db]), device_id_type=pl.DeviceIdType.MESH)
    for dp in (1, 2, 3):
        pl.semaphore_signal(barrier, inc=1, device_id=(prompts[dp], s, b), device_id_type=pl.DeviceIdType.MESH)
    pl.semaphore_wait(barrier, 10)

    def remote(src, dst, send, recv, target):
        return pltpu.make_async_remote_copy(
            src_ref=src,
            dst_ref=dst,
            send_sem=send,
            recv_sem=recv,
            device_id=target,
            device_id_type=pl.DeviceIdType.MESH,
        )

    near = b + 1 - 2 * lax.rem(b, 2)
    inner = 2 - b // 2
    outer = 3 * (1 - b // 2)

    def row_slot(group, quarter):
        return rows.at[pl.ds(pl.multiple_of(group * 512 + quarter * 128, 128), 128)]

    def own_rows(quarter):
        return out_w.at[quarter, :, pl.ds(pl.multiple_of(s * 1024, 1024), 1024)]

    def row_copy(k, target, source):
        return remote(own_rows(p), row_slot(source, p), row_send.at[k], row_recv.at[source], (p, s, target))

    def forward_copy(k, source):
        slot = row_slot(source, p)
        return remote(slot, slot, forward_send.at[k], row_recv.at[source], (p, s, near))

    def share_copy(group, dp, source):
        return remote(
            row_slot(group, source),
            row_slot(group, source),
            share_send.at[group, dp],
            share_recv.at[group, source],
            (prompts[dp], s, b),
        )

    def qkv_copy(g, db, ds, frame, row):
        return remote(
            proj.at[:, blks[db], g, seqs[ds]],
            qkv.at[:, g, :, frame, row],
            qkv_send.at[g, db, ds],
            qkv_recv.at[g, frame, row],
            (p, seqs[ds], blks[db]),
        )

    def res_copy(db, ds, frame, row):
        return remote(
            res_in.at[blks[db], seqs[ds]],
            res.at[:, frame, row],
            res_send.at[db, ds],
            res_recv.at[frame, row],
            (p, seqs[ds], blks[db]),
        )

    def noisy_copy(db, ds, frame, row):
        return remote(
            noisy_in.at[blks[db]],
            noisy.at[frame, row],
            noisy_send.at[db, ds],
            noisy_recv.at[frame, row],
            (p, seqs[ds], blks[db]),
        )

    row_copy(0, inner, b).start()
    row_copy(1, near, b).start()
    for g in range(2):
        for db, ds in pairs:
            qkv_copy(g, db, ds, b, s).start()
    own = [
        pltpu.make_async_copy(proj.at[:, b, g, s], qkv.at[:, g, :, b, s], local_sem.at[g]) for g in range(4)
    ]
    own.append(pltpu.make_async_copy(res_in.at[b, s], res.at[:, b, s], local_sem.at[4]))
    own.append(pltpu.make_async_copy(noisy_in.at[b], noisy.at[b, s], local_sem.at[5]))
    for quarter in range(4):
        own.append(pltpu.make_async_copy(own_rows(quarter), row_slot(b, quarter), local_sem.at[6 + quarter]))
    tables = ((mod_in, mod), (final_in, final_w), (final_b_in, final_b), (conv_in, conv_w), (conv_b_in, conv_b))
    for k, (src, dst) in enumerate(tables):
        own.append(pltpu.make_async_copy(src, dst, local_sem.at[10 + k]))
    for copy in own:
        copy.start()

    def share(source):
        for dp in (1, 2, 3):
            share_copy(source, dp, p).start()

    row_copy(0, near, near).wait_recv()
    share(near)

    @pl.when(lax.rem(b, 3) != 0)
    def _():
        for k, source in enumerate((inner, outer)):
            row_copy(0, near, source).wait_recv()
            forward_copy(k, source).start()
            share(source)

    for db, ds in pairs:
        qkv_copy(2, db, ds, b, s).start()

    for half in range(2):
        at_row = lax.broadcasted_iota(jnp.int32, (256, 768), 0)
        at_col = lax.broadcasted_iota(jnp.int32, (256, 768), 1)
        same = (at_row >> 6) == ((at_col >> 6) & 3)
        place = (at_col & 63) == 2 * (at_row & 31) + (half + 1) - (at_col >> 8)
        spread[half * 256 : half * 256 + 256, :] = jnp.where(same & place, 1.0, 0.0).astype(jnp.bfloat16)
    for copy in own[10:]:
        copy.wait()
    for k in range(3):
        video = lax.broadcasted_iota(jnp.int32, (4, 2048), 0)
        factors[k : k + 1, :] = jnp.sum(jnp.where(video == b, mod[k], 0.0), axis=0, keepdims=True)
    bias[...] = jnp.broadcast_to(conv_b[...], (128, 512)).T

    conv_t[...] = conv_w[...].T

    def split(value):
        high = value.astype(jnp.bfloat16)
        return high.astype(jnp.float32), value - high.astype(jnp.float32)

    row = lax.broadcasted_iota(jnp.int32, (8, 1024), 0)
    tilts = []
    moved = final_b[...]
    for half in range(2):
        lanes = slice(half * 1024, half * 1024 + 1024)
        high, low = split(1.0 + factors[1:2, lanes])
        shift_high, shift_low = split(factors[0:1, lanes])
        parts = jnp.where(row == 0, high, 0.0) + jnp.where(row == 1, low, 0.0)
        parts = parts + jnp.where(row == 2, shift_high, 0.0) + jnp.where(row == 3, shift_low, 0.0)
        sums = dot(parts.astype(jnp.bfloat16), final_w[:, lanes], 1, 1)
        tilts.append(sums[0:1] + sums[1:2])
        moved = moved + sums[2:3] + sums[3:4]
    tilt_mine = jnp.where(s == 0, tilts[0], tilts[1])
    tilt_other = jnp.where(s == 0, tilts[1], tilts[0])

    @pl.when(lax.rem(b, 3) == 0)
    def _():
        for source in (inner, outer):
            row_copy(0, near, source).wait_recv()
            share(source)

    def att_copy(g, side):
        cols = att.at[:, pl.ds(pl.multiple_of((4 * g + 2 * side) * 128, 256), 256)]
        return remote(cols, cols, att_send.at[g], att_recv.at[g], (p, other, b))

    scale = 128 ** (-0.5)
    for g in range(4):
        own[g].wait()
        for db, ds in pairs:
            qkv_copy(g, db, ds, froms[db], seqs[ds]).wait_recv()
        for k in range(2):
            q = qkv[0, g, k].reshape(256, 128)
            key = qkv[1, g, k].reshape(256, 128)
            value = qkv[2, g, k].reshape(256, 128)
            scores = dot(q, key, 1, 1) * scale
            weights = jnp.exp(scores - jnp.max(scores, axis=1, keepdims=True))
            totals = jnp.sum(weights, axis=1, keepdims=True)
            result = (dot(weights.astype(jnp.bfloat16), value) / totals).astype(jnp.bfloat16)
            att[:, pl.ds(pl.multiple_of((4 * g + 2 * s + k) * 128, 128), 128)] = result
        att_copy(g, s).start()
        for db, ds in pairs:
            if g == 0:
                qkv_copy(3, db, ds, b, s).start()
            if g == 2:
                noisy_copy(db, ds, b, s).start()
                res_copy(db, ds, b, s).start()
    for quarter in range(4):
        own[6 + quarter].wait()
    for source in (near, inner, outer):
        for dp in (1, 2, 3):
            share_copy(source, dp, prompt_froms[dp]).wait_recv()
    for done in range(4):
        att_copy(done, other).wait_recv()
    for n in range(2):
        lanes = slice(n * 512, n * 512 + 512)
        projected[:, lanes] = dot(att[...], rows[:, lanes])

    own[4].wait()
    for db, ds in pairs:
        res_copy(db, ds, froms[db], seqs[ds]).wait_recv()
    total = jnp.zeros((256, 128), jnp.float32)
    for h in range(8):
        lanes = slice(h * 128, h * 128 + 128)
        gate = jnp.where(s == 0, factors[2:3, lanes], factors[2:3, 1024 + h * 128 : 1152 + h * 128])
        value = res[h].reshape(256, 128).astype(jnp.float32) + gate * projected[:, lanes]
        projected[:, lanes] = value
        total = total + value
    center = jnp.sum(total, axis=1, keepdims=True) * (1.0 / 1024)
    total = jnp.zeros((256, 128), jnp.float32)
    for h in range(8):
        lanes = slice(h * 128, h * 128 + 128)
        away = projected[:, lanes] - center
        total = total + jnp.square(away)
        gain = jnp.where(s == 0, factors[1:2, lanes], factors[1:2, 1024 + h * 128 : 1152 + h * 128])
        centred[:, lanes] = (away * (1.0 + gain)).astype(jnp.bfloat16)
    squares = jnp.sum(total, axis=1, keepdims=True)
    weighted = dot(centred[...], final_w[:, pl.ds(pl.multiple_of(s * 1024, 1024), 1024)], 1, 1)
    summary_out[:, 0:64] = weighted
    lane = lax.broadcasted_iota(jnp.int32, (256, 64), 1)
    summary_out[:, 64:128] = jnp.where(lane == 0, center, jnp.where(lane == 1, squares, 0.0))
    summary = remote(summary_out, summary_in, summary_sem.at[0], summary_sem.at[1], (p, other, b))
    summary.start()
    own[5].wait()
    for db, ds in pairs:
        noisy_copy(db, ds, froms[db], seqs[ds]).wait_recv()
    start = noisy[...].reshape(256, 64)
    summary.wait_recv()
    center_other = summary_in[:, 64:65]
    squares = squares + summary_in[:, 65:66]
    apart = (center - center_other) * 0.5
    inverse = lax.rsqrt(squares * (1.0 / 2048) + jnp.square(apart) + 1e-06)
    weighted = weighted + summary_in[:, 0:64] + apart * (tilt_mine - tilt_other)
    prediction = inverse * weighted + moved
    latents = ((start + step[b] * prediction) / 0.476986).astype(jnp.bfloat16)

    to = lax.broadcasted_iota(jnp.int32, (64, 64), 0)
    channel = lax.broadcasted_iota(jnp.int32, (64, 64), 1)
    pick = jnp.where(channel == 4 * (to & 15) + (to >> 4), 1.0, 0.0).astype(jnp.bfloat16)
    image = dot(pick, latents, 1, 1)
    row_of = (lax.broadcasted_iota(jnp.int32, (16, 256), 1) >> 5) & 1
    for r in range(4):
        here = row_of == s + (r + 1) // 2 - 1
        for half in range(2):
            at = (1 - r % 2) * 32 + half * 16
            kept = jnp.where(here, image[at : at + 16], 0.0).astype(jnp.bfloat16)
            strip[r * 16 : r * 16 + 16, half * 256 : half * 256 + 256] = kept
    shifted = dot(strip[...], spread[...])
    for e in range(3):
        for f in range(4):
            lanes = slice(e * 256 + f * 64, e * 256 + f * 64 + 64)
            block = jnp.concatenate([shifted[0:48, lanes], shifted[16:64, lanes]], axis=1).astype(jnp.bfloat16)
            for t in range(3):
                for frame in range(4):
                    if max(frame + t - 2, 0) == f:
                        for y in range(3):
                            at = (t * 9 + y * 3 + e) * 16
                            columns[at : at + 16, frame * 128 : frame * 128 + 128] = block[y * 16 : y * 16 + 16]
    for f in range(4):
        decoded = dot(conv_t[...], columns[:, f * 128 : f * 128 + 128])
        out[f] = (decoded + bias[...]).astype(jnp.bfloat16)

    for k, source in enumerate((near, inner, outer)):
        if k < 2:
            row_copy(k, near, b).wait_send()
        else:

            @pl.when(lax.rem(b, 3) != 0)
            def _():
                forward_copy(0, inner).wait_send()
                forward_copy(1, outer).wait_send()

        for dp in (1, 2, 3):
            share_copy(source, dp, p).wait_send()
    for db, ds in pairs:
        res_copy(db, ds, b, s).wait_send()
        noisy_copy(db, ds, b, s).wait_send()
        for g in range(4):
            qkv_copy(g, db, ds, b, s).wait_send()
    for g in range(4):
        att_copy(g, s).wait_send()
    summary.wait_send()


def fused(
    projections,
    residual,
    out_proj,
    modulation,
    final_weight,
    final_bias,
    noisy_latents,
    step_size,
    conv_weight,
    conv_bias,
):
    anywhere = pl.BlockSpec(memory_space=pl.ANY)
    vmem = pl.BlockSpec(memory_space=pltpu.VMEM)
    smem = pl.BlockSpec(memory_space=pltpu.SMEM)
    half, full = jnp.bfloat16, jnp.float32
    dma = pltpu.SemaphoreType.DMA
    decoded = pl.pallas_call(
        fused_kernel,
        out_shape=jax.ShapeDtypeStruct((4, 512, 128), half),
        in_specs=[anywhere] * 9 + [smem],
        out_specs=vmem,
        scratch_shapes=[
            pltpu.VMEM((3, 4, 2, 4, 2, 32, 128), half),
            pltpu.VMEM((8, 4, 2, 32, 128), half),
            pltpu.VMEM((4, 2, 32, 64), full),
            pltpu.VMEM((2048, 1024), half),
            pltpu.VMEM((256, 2048), half),
            pltpu.VMEM((256, 1024), full),
            pltpu.VMEM((256, 1024), half),
            pltpu.VMEM((256, 128), full),
            pltpu.VMEM((256, 128), full),
            pltpu.VMEM((64, 512), half),
            pltpu.VMEM((512, 768), half),
            pltpu.VMEM((432, 512), half),
            pltpu.VMEM((512, 128), full),
            pltpu.VMEM((8, 2048), full),
            pltpu.VMEM((3, 4, 2048), full),
            pltpu.VMEM((64, 2048), half),
            pltpu.VMEM((1, 64), full),
            pltpu.VMEM((432, 512), half),
            pltpu.VMEM((1, 512), full),
            pltpu.VMEM((512, 432), half),
            dma((4, 4, 2)),
            dma((4, 4, 2)),
            dma((4, 2)),
            dma((4, 2)),
            dma((4, 2)),
            dma((4, 2)),
            dma((2,)),
            dma((4,)),
            dma((2,)),
            dma((4, 4)),
            dma((4, 4)),
            dma((4,)),
            dma((4,)),
            dma((2,)),
            dma((15,)),
        ],
        compiler_params=pltpu.CompilerParams(
            collective_id=0, has_side_effects=True, vmem_limit_bytes=60 * 1024 * 1024
        ),
    )(
        projections.reshape(3, 4, 4, 2, 2, 32, 128),
        residual.reshape(4, 2, 8, 32, 128),
        out_proj.reshape(4, 128, 2048),
        noisy_latents.reshape(4, 32, 64),
        modulation,
        final_weight.T,
        final_bias.reshape(1, 64),
        conv_weight.reshape(432, 512),
        conv_bias.reshape(1, 512),
        step_size,
    )
    return decoded[None]


def solution(mesh):
    return jax.shard_map(
        fused if fits(mesh) else body,
        mesh=mesh,
        in_specs=(
            P(None, None, None, "blk", "seq", None),
            P(None, None, "blk", "seq", None),
            P("blk", None),
            P(),
            P(),
            P(),
            P(None, "blk", "seq", None),
            P(),
            P(),
            P(),
        ),
        out_specs=P(("prompt", "blk"), None, None, "seq"),
        check_vma=False,
    )
```
